256 devices in a mesh: space: 128 (over y, x, z), coarse: 2 (over core).
Axes of the slice: x: 4, y: 4, z: 8, core: 2. Of those that a mesh axis runs over, the one named last changes fastest.
Arguments:
- cells: float32 [131072, 128], P('space'), may hold values from -6 to 6
- w_send: float32 [128, 128], replicated, may hold values from -0.5 to 0.5
- w_recv: float32 [128, 128], replicated, may hold values from -0.5 to 0.5
- w_msg: float32 [128, 128], replicated, may hold values from -0.5 to 0.5
- w_coarse: float32 [128, 128], replicated, may hold values from -0.5 to 0.5
- w_self: float32 [128, 128], replicated, may hold values from -0.5 to 0.5
- w_agg: float32 [128, 128], replicated, may hold values from -0.5 to 0.5
- w_up: float32 [128, 128], replicated, may hold values from -0.5 to 0.5
- w_out: float32 [128, 128], replicated, may hold values from -0.5 to 0.5
- upstream: float32 [131072, 128], P('space'), may hold values from -6 to 6
- senders: int32 [786432], P(('space', 'coarse')), may hold values from 0 to 2047
- receivers: int32 [786432], P(('space', 'coarse')), may hold values from 0 to 1023
- send_map: int32 [128, 4, 256], P('space'), may hold values from 0 to 1023
- pool_map: int32 [131072], P('space'), may hold values from 0 to 2047, as said below
- coarse_senders: int32 [12288], P('coarse'), may hold values from 0 to 2047
- coarse_receivers: int32 [12288], P('coarse'), may hold values from 0 to 1023
Outputs:
- d_cells: float32 [131072, 128], P('space')
- weight_grads: float32 [8, 128, 128], replicated
The draws below stay inside these ranges and needn't reach their ends.
Inputs may be any that keep to these rules, and one draw needn't show every extreme that they name: `pool_map`: the cells of block d map to coarse nodes d * 16 to d * 16 + 2 * 16 - 1, taken modulo 2048.
All inputs are finite; a program needn't handle non-finite values.
Results may differ from the reference program's by a relative error of at most 0.00014.
Values sent between devices are 32-bit elements; how exact they have to be, the bound alone decides.
No kernel may reach another device: no remote copies, remote signals or barrier semaphores. Data moves between devices by JAX's collectives and lax.ppermute only.
A program may use at most 128 MiB of HBM per device.

```python
import jax
import jax.numpy as jnp
from jax import lax

LATENT = 128
CELL_DEV = 1024
SLOTS = 256
COARSE_DEV = 16
CELLS = 131072
COARSE = 2048
EDGES = 786432
N_SPACE = 128
N_COARSE = 2


def draw_pool_map(key, part):
    key = jax.random.fold_in(key, 5)
    cell_index = jnp.arange(CELL_DEV * N_SPACE, dtype=jnp.int32)
    base = cell_index // CELL_DEV * COARSE_DEV
    jitter = jax.random.randint(key, (CELL_DEV * N_SPACE,), 0, 2 * COARSE_DEV, dtype=jnp.int32)
    return ((base + jitter) % COARSE).astype(jnp.int32)


def with_ends(drawn, own_key, low, high):
    longest = drawn.shape.index(max(drawn.shape))
    spots = []
    for shift in (0, 1):
        where = [jax.random.randint(jax.random.fold_in(own_key, axis), (), 0, length) for axis, length in enumerate(drawn.shape)]
        where[longest] = (where[longest] + shift) % drawn.shape[longest]
        spots.append(tuple(where))
    return drawn.at[spots[0]].set(low).at[spots[1]].set(high)


def steps_of(rng, dims, cuts, least, top_value):
    gain = 1.0
    for dim, parts in cuts:
        heights = jax.random.uniform(jax.random.fold_in(jax.random.fold_in(rng, 6), dim), (parts,), jnp.float32, least / len(cuts), top_value / len(cuts))
        gain = gain * jnp.repeat(jnp.exp(heights), dims[dim] // parts).reshape((-1,) + (1,) * (len(dims) - 1 - dim))
    return gain


def scatter_about(key, shape, width, limit, split=(), kind=jnp.bfloat16):
    drawn = jax.random.normal(key, shape, jnp.float32) * width
    if len(split) > 0:
        drawn = steps_of(key, shape, split, -0.22, 0.18) * drawn
    return jnp.clip(drawn, min=-limit, max=limit).astype(kind)


def setup_inputs(seed: int = 0) -> dict:
    streams_of = jax.random.split(jax.random.key(seed), 17)
    cells = scatter_about(streams_of[0], (CELLS, LATENT), 1.0, 6.0, ((0, 128),), jnp.float32)
    w_send = scatter_about(streams_of[1], (LATENT, LATENT), LATENT ** -0.5, 0.5, (), jnp.float32)
    w_recv = scatter_about(streams_of[2], (LATENT, LATENT), LATENT ** -0.5, 0.5, (), jnp.float32)
    w_msg = scatter_about(streams_of[3], (LATENT, LATENT), LATENT ** -0.5, 0.5, (), jnp.float32)
    w_coarse = scatter_about(streams_of[4], (LATENT, LATENT), LATENT ** -0.5, 0.5, (), jnp.float32)
    w_self = scatter_about(streams_of[5], (LATENT, LATENT), LATENT ** -0.5, 0.5, (), jnp.float32)
    w_agg = scatter_about(streams_of[6], (LATENT, LATENT), LATENT ** -0.5, 0.5, (), jnp.float32)
    w_up = scatter_about(streams_of[7], (LATENT, LATENT), LATENT ** -0.5, 0.5, (), jnp.float32)
    w_out = scatter_about(streams_of[8], (LATENT, LATENT), LATENT ** -0.5, 0.5, (), jnp.float32)
    upstream = scatter_about(streams_of[9], (CELLS, LATENT), 1.0, 6.0, ((0, 128),), jnp.float32)
    senders = with_ends(jax.random.randint(streams_of[10], (EDGES,), 0, CELL_DEV + 4 * SLOTS), jax.random.fold_in(streams_of[10], 1), 0, (CELL_DEV + 4 * SLOTS) - 1).astype(jnp.int32)
    receivers = with_ends(jax.random.randint(streams_of[11], (EDGES,), 0, CELL_DEV), jax.random.fold_in(streams_of[11], 1), 0, CELL_DEV - 1).astype(jnp.int32)
    send_map = with_ends(jax.random.randint(streams_of[12], (N_SPACE, 4, SLOTS), 0, CELL_DEV), jax.random.fold_in(streams_of[12], 1), 0, CELL_DEV - 1).astype(jnp.int32)
    pool_map = draw_pool_map(jax.random.fold_in(streams_of[16], 71), 0)
    coarse_senders = with_ends(jax.random.randint(streams_of[14], (6 * COARSE,), 0, COARSE), jax.random.fold_in(streams_of[14], 1), 0, COARSE - 1).astype(jnp.int32)
    coarse_receivers = with_ends(jax.random.randint(streams_of[15], (6 * COARSE,), 0, COARSE // N_COARSE), jax.random.fold_in(streams_of[15], 1), 0, (COARSE // N_COARSE) - 1).astype(jnp.int32)
    return dict(cells=cells, w_send=w_send, w_recv=w_recv, w_msg=w_msg, w_coarse=w_coarse, w_self=w_self, w_agg=w_agg, w_up=w_up, w_out=w_out, upstream=upstream, senders=senders, receivers=receivers, send_map=send_map, pool_map=pool_map, coarse_senders=coarse_senders, coarse_receivers=coarse_receivers)


OFFSETS = (1, -1, 2, -2)
EPSILON = 1e-05

def matmul(left, right):
    return jnp.dot(left, right, precision=lax.Precision.HIGHEST)

def layer_norm(values):
    centered = values - lax.optimization_barrier(jnp.mean(values, axis=-1, keepdims=True))
    variance = lax.optimization_barrier(jnp.mean(centered * centered, axis=-1, keepdims=True))
    return centered * lax.rsqrt(variance + EPSILON)

def edge_messages(cell_table, cell_rows, w_first, w_second, w_third, edge_senders, edge_receivers):
    pre_act = matmul(cell_table[edge_senders], w_first) + matmul(cell_rows[edge_receivers], w_second)
    message = layer_norm(matmul(jax.nn.silu(pre_act), w_third))
    return jax.ops.segment_sum(message, edge_receivers, num_segments=cell_rows.shape[0])

def node_update(cell_rows, aggregate, lifted, w_self, w_agg, w_up, w_out):
    inner_sum = matmul(cell_rows, w_self) + matmul(aggregate, w_agg) + matmul(lifted, w_up)
    return cell_rows + layer_norm(matmul(jax.nn.silu(inner_sum), w_out))

def coarse_update(pooled_all, own_rows, w_coarse, coarse_senders, coarse_receivers):
    gathered = jax.ops.segment_sum(pooled_all[coarse_senders], coarse_receivers, num_segments=own_rows.shape[0])
    return own_rows + jax.nn.silu(matmul(own_rows + gathered, w_coarse))

def forward(cells, weights, senders, receivers, send_map, pool_map, coarse_senders, coarse_receivers):
    w_send, w_recv, w_msg, w_coarse, w_self, w_agg, w_up, w_out = weights
    blocks = cells.reshape(N_SPACE, CELL_DEV, LATENT)
    device = jnp.arange(N_SPACE, dtype=jnp.int32)
    pieces = [blocks]
    for group_index, offset in enumerate(OFFSETS):
        source = device - offset
        inside = (source >= 0) & (source < N_SPACE)
        clipped = jnp.clip(source, 0, N_SPACE - 1).astype(jnp.int32)
        picked = blocks[clipped[:, None], send_map[clipped, group_index]]
        pieces.append(jnp.where(inside[:, None, None], picked, jnp.zeros_like(picked)))
    tables = jnp.concatenate(pieces, axis=1)
    edge_senders = senders.reshape(N_SPACE, -1)
    edge_receivers = receivers.reshape(N_SPACE, -1)
    aggregate = jax.vmap(edge_messages, in_axes=(0, 0, None, None, None, 0, 0))(tables, blocks, w_send, w_recv, w_msg, edge_senders, edge_receivers)
    aggregate = aggregate.reshape(CELL_DEV * N_SPACE, LATENT)
    pool_scale = (COARSE_DEV / CELL_DEV) ** 0.5
    pooled = jax.ops.segment_sum(cells, pool_map, num_segments=COARSE) * pool_scale
    owner = jnp.arange(6 * COARSE, dtype=jnp.int32) // (3 * COARSE)
    global_receivers = owner * (COARSE // N_COARSE) + coarse_receivers
    coarse_new = coarse_update(pooled, pooled, w_coarse, coarse_senders, global_receivers)
    return node_update(cells, aggregate, coarse_new[pool_map], w_self, w_agg, w_up, w_out)

def reference(cells, w_send, w_recv, w_msg, w_coarse, w_self, w_agg, w_up, w_out, upstream, senders, receivers, send_map, pool_map, coarse_senders, coarse_receivers):

    def apply_step(cell_values, weights):
        return forward(cell_values, weights, senders, receivers, send_map, pool_map, coarse_senders, coarse_receivers)
    weights = (w_send, w_recv, w_msg, w_coarse, w_self, w_agg, w_up, w_out)
    updated, pullback = jax.vjp(apply_step, cells, weights)
    d_cells, d_weights = pullback(upstream)
    grad_scale = (CELL_DEV * N_SPACE) ** (-0.5)
    return (d_cells, jnp.stack(d_weights) * grad_scale)
```

```python
import functools

import jax
import jax.numpy as jnp
from jax import lax
from jax.experimental import pallas as pl
from jax.experimental.pallas import tpu as pltpu
from jax.sharding import PartitionSpec as P

EPSILON = 1e-05
LANES = 128
TILE = 512
F32 = jnp.float32
BF16 = jnp.bfloat16
VMEM_LIMIT = 48 * 1024 * 1024


def split(values):
    high = values.astype(BF16)
    low = (values - high.astype(F32)).astype(BF16)
    return jnp.concatenate([high, low], axis=1)


def fold(values):
    return values[:, :LANES] + values[:, LANES:]


def weight_pair(weight):
    pair = split(weight)
    return jnp.concatenate([pair, pair], axis=0)


def weight_pair_t(weight):
    high = weight.astype(BF16)
    low = (weight - high.astype(F32)).astype(BF16)
    stacked = jnp.concatenate([high, low], axis=0)
    return jnp.concatenate([stacked, stacked], axis=1)


def mm(left, right):
    return lax.dot_general(left, right, (((1,), (0,)), ((), ())), preferred_element_type=F32)


def mm_t(left, right):
    return lax.dot_general(left, right, (((1,), (1,)), ((), ())), preferred_element_type=F32)


def tm_m(left, right):
    return lax.dot_general(left, right, (((0,), (0,)), ((), ())), preferred_element_type=F32)


def outer(left_pair, right_pair):
    full = tm_m(left_pair, right_pair)
    return fold(full[:LANES] + full[LANES:])


def as_column(row):
    return jnp.transpose(jnp.broadcast_to(row, (LANES, LANES)))


def one_hot_rows(row, count):
    column = jnp.concatenate([as_column(row).astype(jnp.int16)] * (count // LANES), axis=1)
    place = lax.broadcasted_iota(jnp.int16, (LANES, count), 1)
    return jnp.where(column == place, jnp.ones((), BF16), jnp.zeros((), BF16))


def one_hot_columns(row, first, count):
    wide = jnp.broadcast_to(row - first, (16, LANES)).astype(jnp.int16)
    wide = jnp.concatenate([wide] * (count // 16), axis=0)
    place = lax.broadcasted_iota(jnp.int16, (count, LANES), 0)
    return jnp.where(wide == place, jnp.ones((), BF16), jnp.zeros((), BF16))


def norm_parts(values):
    centered = values - jnp.mean(values, axis=-1, keepdims=True)
    variance = jnp.mean(centered * centered, axis=-1, keepdims=True)
    scale = lax.rsqrt(variance + EPSILON)
    return centered * scale, scale


def norm_back(normed, scale, cotangent):
    shared = cotangent - normed * jnp.mean(cotangent * normed, axis=-1, keepdims=True)
    return scale * (shared - jnp.mean(shared, axis=-1, keepdims=True))


def sigmoid(values):
    return 1.0 / (1.0 + jnp.exp(-values))


def silu_slope(values, gate):
    return gate * (1.0 + values * (1.0 - gate))


def relative_pool(row, place, coarse_block, coarse_total):
    shifted = row - place * coarse_block
    return jnp.where(shifted < 0, shifted + coarse_total, shifted)


def pack_kernel(sizes, place_ref, cells_ref, send_ref, pool_ref, near_ref, far_ref, pool_out):
    coarse_block, coarse_total, scale = sizes
    core = place_ref[1]
    count = cells_ref.shape[0]
    pair = split(cells_ref[...])
    hot = []
    for chunk in range(count // LANES):
        row = relative_pool(pool_ref[chunk : chunk + 1, :], place_ref[0], coarse_block, coarse_total)
        hot.append(one_hot_columns(row, 0, 2 * coarse_block))
    pool_out[...] = fold(mm(jnp.concatenate(hot, axis=1), pair)) * scale
    per = send_ref.shape[0] // 4
    for group, out in ((0, near_ref), (1, far_ref)):
        for chunk in range(per):
            row = send_ref[pl.ds(group * 2 * per + core * per + chunk, 1), :]
            out[chunk * LANES : (chunk + 1) * LANES, :] = fold(mm(one_hot_rows(row, count), pair))


def sender_row(row, core, count, slots):
    return jnp.where(row >= count, row ^ (core * slots), row)


def edge_kernel(
    place_ref,
    cells_ref,
    near_ref,
    near_other_ref,
    far_ref,
    far_other_ref,
    w_send_ref,
    w_recv_ref,
    w_msg_ref,
    send_ref,
    recv_ref,
    pre_ref,
    hidden_ref,
    agg_ref,
    table,
    hot,
    normed,
):
    core = place_ref[1]
    count = cells_ref.shape[0]
    slots = near_ref.shape[0]
    nodes = 2 * count + 4 * slots
    edges = pre_ref.shape[0]
    w_send = weight_pair(w_send_ref[...])
    cells_pair = split(cells_ref[...])
    table[:count, :] = split(fold(mm(cells_pair, w_send)))
    for spot, part in enumerate((near_ref, near_other_ref, far_ref, far_other_ref)):
        start = count + spot * slots
        table[start : start + slots, :] = split(fold(mm(split(part[...]), w_send)))
    table[nodes - count :, :] = split(fold(mm(cells_pair, weight_pair(w_recv_ref[...]))))
    w_msg = weight_pair(w_msg_ref[...])
    chunks = TILE // LANES

    def tile(step, carry):
        start = pl.multiple_of(step * TILE, TILE)
        for chunk in range(chunks):
            place = step * chunks + chunk
            row = sender_row(send_ref[pl.ds(place, 1), :], core, count, slots)
            hot[chunk * LANES : (chunk + 1) * LANES, : nodes - count] = one_hot_rows(row, nodes - count)
            row = recv_ref[pl.ds(place, 1), :]
            hot[chunk * LANES : (chunk + 1) * LANES, nodes - count :] = one_hot_rows(row, count)
        pre = fold(mm(hot[...], table[...]))
        pre_ref[pl.ds(start, TILE), :] = pre
        hidden = fold(mm(split(pre * sigmoid(pre)), w_msg))
        hidden_ref[pl.ds(start, TILE), :] = hidden
        normed[pl.ds(start, TILE), :] = split(norm_parts(hidden)[0])
        return carry

    lax.fori_loop(0, edges // TILE, tile, 0)
    part = 256

    def gather_tile(step, carry):
        first = step * part
        across = [
            one_hot_columns(recv_ref[chunk : chunk + 1, :], first, part)
            for chunk in range(edges // LANES)
        ]
        agg_ref[pl.ds(pl.multiple_of(first, part), part), :] = fold(
            mm(jnp.concatenate(across, axis=1), normed[...])
        )
        return carry

    lax.fori_loop(0, count // part, gather_tile, 0)


def count_kernel(
    sizes, place_ref, send_ref, send_other_ref, recv_ref, recv_other_ref, into_ref, from_ref
):
    coarse_block, coarse_total = sizes
    core = place_ref[1]
    rows = 2 * coarse_block
    half = coarse_block // 2
    own = coarse_total // 2
    into_ref[...] = jnp.zeros_like(into_ref)
    from_ref[...] = jnp.zeros_like(from_ref)
    groups = into_ref.shape[0]
    chunks = send_ref.shape[0]
    batch = 8

    def parts(node):
        near = relative_pool(node, place_ref[0], coarse_block, coarse_total)
        inside = node & (coarse_block - 1)
        column = (node // coarse_block) * half + (inside & (half - 1))
        held = (inside // half) == core
        return near, column, held

    def tally(near, column, held):
        wanted = jnp.where(held & (near < rows), (column // LANES) * rows + near, -1)
        return wanted, column & (LANES - 1)

    for senders, receivers, owner in (
        (send_ref, recv_ref, core),
        (send_other_ref, recv_other_ref, 1 - core),
    ):

        def step(index, carry, senders=senders, receivers=receivers, owner=owner):
            first, second, third, fourth = [], [], [], []
            for chunk in range(batch):
                place = index * batch + chunk
                sender = senders[pl.ds(place, 1), :]
                receiver = receivers[pl.ds(place, 1), :] + owner * own
                sender_near, sender_column, sender_held = parts(sender)
                receiver_near, receiver_column, receiver_held = parts(receiver)
                wanted, low = tally(receiver_near, sender_column, sender_held)
                first.append(one_hot_columns(wanted, 0, groups))
                second.append(one_hot_columns(low, 0, LANES))
                wanted, low = tally(sender_near, receiver_column, receiver_held)
                third.append(one_hot_columns(wanted, 0, groups))
                fourth.append(one_hot_columns(low, 0, LANES))
            into_ref[...] += mm_t(jnp.concatenate(first, axis=1), jnp.concatenate(second, axis=1))
            from_ref[...] += mm_t(jnp.concatenate(third, axis=1), jnp.concatenate(fourth, axis=1))
            return carry

        lax.fori_loop(0, chunks // batch, step, 0)


def weigh_counts(count_ref, values_ref, rows):
    total = jnp.zeros((rows, LANES), F32)
    for group in range(count_ref.shape[0] // rows):
        total += jnp.dot(
            count_ref[group * rows : (group + 1) * rows, :],
            values_ref[group * LANES : (group + 1) * LANES, :],
            precision=lax.Precision.HIGHEST,
            preferred_element_type=F32,
        )
    return total


def coarse_sum_kernel(sizes, place_ref, count_ref, values_ref, sums_ref):
    coarse_block, blocks = sizes
    rows = 2 * coarse_block
    half = coarse_block // 2
    place, core = place_ref[0], place_ref[1]
    after = lax.rem(place + 1, blocks)
    sums_ref[:rows, :] = weigh_counts(count_ref, values_ref, rows)
    sums_ref[rows:, :] = jnp.zeros((rows, LANES), F32)
    for spot, block in ((0, place), (1, after)):
        own = values_ref[pl.ds(pl.multiple_of(block * half, half), half), :]
        sums_ref[pl.ds(pl.multiple_of(rows + spot * coarse_block + core * half, half), half), :] = own


def coarse_back_sum_kernel(rows, count_ref, values_ref, sums_ref):
    sums_ref[...] = weigh_counts(count_ref, values_ref, rows)


def node_kernel(
    sizes,
    place_ref,
    cells_ref,
    agg_ref,
    agg_other_ref,
    sums_ref,
    sums_other_ref,
    upstream_ref,
    pool_ref,
    w_coarse_ref,
    w_self_ref,
    w_agg_ref,
    w_up_ref,
    w_out_ref,
    d_agg_ref,
    d_direct_ref,
    d_coarse_ref,
    coarse_in_ref,
    grads_ref,
    g_self,
    g_agg,
    g_out,
    lifted_back,
):
    coarse_block, coarse_total = sizes
    rows = 2 * coarse_block
    count = cells_ref.shape[0]
    sums = sums_ref[...] + sums_other_ref[...]
    pooled = sums[rows:]
    coarse_in = pooled + sums[:rows]
    coarse_in_ref[...] = coarse_in
    coarse_pre = fold(mm(split(coarse_in), weight_pair(w_coarse_ref[...])))
    coarse_new = pooled + coarse_pre * sigmoid(coarse_pre)
    raised = fold(mm(split(coarse_new), weight_pair(w_up_ref[...])))
    raised = split(jnp.concatenate([raised, jnp.zeros((LANES - rows, LANES), F32)], axis=0))
    w_self, w_agg, w_out = w_self_ref[...], w_agg_ref[...], w_out_ref[...]
    self_pair, agg_pair, out_pair = weight_pair(w_self), weight_pair(w_agg), weight_pair(w_out)
    self_back, agg_back, out_back = weight_pair_t(w_self), weight_pair_t(w_agg), weight_pair_t(w_out)
    part = 256
    g_self[...] = jnp.zeros_like(g_self)
    g_agg[...] = jnp.zeros_like(g_agg)
    g_out[...] = jnp.zeros_like(g_out)
    lifted_back[...] = jnp.zeros_like(lifted_back)

    def tile(step, carry):
        at = pl.ds(pl.multiple_of(step * part, part), part)
        cells_pair = split(cells_ref[at, :])
        agg_pair_rows = split(agg_ref[at, :] + agg_other_ref[at, :])
        down, across = [], []
        for chunk in range(part // LANES):
            row = pool_ref[pl.ds(step * (part // LANES) + chunk, 1), :]
            row = relative_pool(row, place_ref[0], coarse_block, coarse_total)
            down.append(one_hot_rows(row, LANES))
            across.append(one_hot_columns(row, 0, rows))
        inner = fold(
            mm(cells_pair, self_pair)
            + mm(agg_pair_rows, agg_pair)
            + mm(jnp.concatenate(down, axis=0), raised)
        )
        gate = sigmoid(inner)
        active = split(inner * gate)
        normed, scale = norm_parts(fold(mm(active, out_pair)))
        upstream = upstream_ref[at, :]
        d_hidden = split(norm_back(normed, scale, upstream))
        g_out[...] += tm_m(active, d_hidden)
        d_inner = fold(mm_t(d_hidden, out_back)) * silu_slope(inner, gate)
        d_pair = split(d_inner)
        d_agg_ref[at, :] = fold(mm_t(d_pair, agg_back))
        d_direct_ref[at, :] = upstream + fold(mm_t(d_pair, self_back))
        g_self[...] += tm_m(cells_pair, d_pair)
        g_agg[...] += tm_m(agg_pair_rows, d_pair)
        lifted_back[...] += mm(jnp.concatenate(across, axis=1), d_pair)
        return carry

    lax.fori_loop(0, count // part, tile, 0)

    def combine(full):
        return fold(full[:LANES] + full[LANES:])

    inner_sums = split(fold(lifted_back[...]))
    d_coarse_ref[...] = fold(mm_t(inner_sums, weight_pair_t(w_up_ref[...])))
    grads_ref[0] = combine(g_self[...])
    grads_ref[1] = combine(g_agg[...])
    grads_ref[2] = outer(split(coarse_new), inner_sums)
    grads_ref[3] = combine(g_out[...])


def coarse_back_kernel(
    coarse_block, place_ref, own_ref, before_ref, coarse_in_ref, w_coarse_ref, base_ref, send_ref, g_ref
):
    half = coarse_block // 2
    core = place_ref[1]
    coarse_in = split(coarse_in_ref[:coarse_block, :])
    weight = w_coarse_ref[...]
    pre = fold(mm(coarse_in, weight_pair(weight)))
    d_coarse = own_ref[:coarse_block, :] + before_ref[...]
    d_pre = split(d_coarse * silu_slope(pre, sigmoid(pre)))
    d_in = fold(mm_t(d_pre, weight_pair_t(weight)))
    base_ref[...] = d_coarse + d_in
    send_ref[...] = jnp.where(core == 0, d_in[:half], d_in[half:])
    g_ref[...] = outer(coarse_in, d_pre)


def edge_back_kernel(
    place_ref,
    cells_ref,
    near_ref,
    near_other_ref,
    far_ref,
    far_other_ref,
    w_send_ref,
    w_recv_ref,
    w_msg_ref,
    send_ref,
    recv_ref,
    pre_ref,
    hidden_ref,
    d_agg_ref,
    near_back,
    near_other_back,
    far_back,
    far_other_back,
    d_cells_ref,
    grads_ref,
    d_agg,
    hot,
    d_pre,
    d_table,
    g_msg,
):
    core = place_ref[1]
    count = cells_ref.shape[0]
    slots = near_ref.shape[0]
    nodes = 2 * count + 4 * slots
    edges = pre_ref.shape[0]
    chunks = TILE // LANES
    d_agg[...] = split(d_agg_ref[...])
    msg_back = weight_pair_t(w_msg_ref[...])
    g_msg[...] = jnp.zeros_like(g_msg)

    def tile(step, carry):
        at = pl.ds(pl.multiple_of(step * TILE, TILE), TILE)
        for chunk in range(chunks):
            row = recv_ref[pl.ds(step * chunks + chunk, 1), :]
            hot[chunk * LANES : (chunk + 1) * LANES, :] = one_hot_rows(row, count)
        normed, scale = norm_parts(hidden_ref[at, :])
        d_hidden = split(norm_back(normed, scale, fold(mm(hot[...], d_agg[...]))))
        pre = pre_ref[at, :]
        gate = sigmoid(pre)
        g_msg[...] += tm_m(split(pre * gate), d_hidden)
        d_pre[at, :] = split(fold(mm_t(d_hidden, msg_back)) * silu_slope(pre, gate))
        return carry

    lax.fori_loop(0, edges // TILE, tile, 0)
    part = 256

    def scatter_tile(step, carry):
        first = step * part
        own = first < nodes - count
        across = []
        for chunk in range(edges // LANES):
            sender = sender_row(send_ref[chunk : chunk + 1, :], core, count, slots)
            receiver = recv_ref[chunk : chunk + 1, :] + (nodes - count)
            across.append(one_hot_columns(jnp.where(own, sender, receiver), first, part))
        d_table[pl.ds(pl.multiple_of(first, part), part), :] = split(
            fold(mm(jnp.concatenate(across, axis=1), d_pre[...]))
        )
        return carry

    lax.fori_loop(0, nodes // part, scatter_tile, 0)
    send_back = weight_pair_t(w_send_ref[...])
    cells_pair = split(cells_ref[...])
    g_send = tm_m(cells_pair, d_table[:count, :])
    for spot, (part_ref, back) in enumerate(
        (
            (near_ref, near_back),
            (near_other_ref, near_other_back),
            (far_ref, far_back),
            (far_other_ref, far_other_back),
        )
    ):
        start = count + spot * slots
        piece = d_table[start : start + slots, :]
        back[...] = fold(mm_t(piece, send_back))
        g_send += tm_m(split(part_ref[...]), piece)
    from_recv = d_table[nodes - count :, :]
    d_cells_ref[...] = fold(
        mm_t(d_table[:count, :], send_back) + mm_t(from_recv, weight_pair_t(w_recv_ref[...]))
    )

    def combine(full):
        return fold(full[:LANES] + full[LANES:])

    grads_ref[0] = combine(g_send)
    grads_ref[1] = outer(cells_pair, from_recv)
    grads_ref[2] = combine(g_msg[...])


def finish_kernel(
    sizes,
    place_ref,
    direct_ref,
    own_ref,
    other_ref,
    near_ref,
    near_other_ref,
    far_ref,
    far_other_ref,
    base_ref,
    base_after_ref,
    sums_ref,
    sums_other_ref,
    send_ref,
    pool_ref,
    out_ref,
):
    coarse_block, coarse_total, scale = sizes
    rows = 2 * coarse_block
    core = place_ref[1]
    count = direct_ref.shape[0]
    pooled = jnp.concatenate([base_ref[...], base_after_ref[...]], axis=0)
    pooled = (pooled + sums_ref[...] + sums_other_ref[...]) * scale
    pooled = split(jnp.concatenate([pooled, jnp.zeros((LANES - rows, LANES), F32)], axis=0))
    returned = split(
        jnp.concatenate([near_ref[...], near_other_ref[...], far_ref[...], far_other_ref[...]], axis=0)
    )
    per = send_ref.shape[0] // 4
    part = 256

    def tile(step, carry):
        first = step * part
        at = pl.ds(pl.multiple_of(first, part), part)
        across = []
        for group, place in ((0, core), (0, 1 - core), (1, core), (1, 1 - core)):
            for chunk in range(per):
                row = send_ref[pl.ds(group * 2 * per + place * per + chunk, 1), :]
                across.append(one_hot_columns(row, first, part))
        down = []
        for chunk in range(part // LANES):
            row = pool_ref[pl.ds(step * (part // LANES) + chunk, 1), :]
            row = relative_pool(row, place_ref[0], coarse_block, coarse_total)
            down.append(one_hot_rows(row, LANES))
        added = mm(jnp.concatenate(across, axis=1), returned) + mm(
            jnp.concatenate(down, axis=0), pooled
        )
        out_ref[at, :] = direct_ref[at, :] + own_ref[at, :] + other_ref[at, :] + fold(added)
        return carry

    lax.fori_loop(0, count // part, tile, 0)


def call(kernel, outs, scratch, flops, name, *operands):
    whole = pl.BlockSpec(memory_space=pltpu.VMEM)
    specs = [pl.BlockSpec(memory_space=pltpu.SMEM) if o.ndim == 1 else whole for o in operands]
    size = sum(o.size * 4 for o in operands) + sum(o.size * 4 for o in outs)
    return pl.pallas_call(
        kernel,
        out_shape=outs,
        in_specs=specs,
        out_specs=[whole] * len(outs),
        scratch_shapes=scratch,
        compiler_params=pltpu.CompilerParams(vmem_limit_bytes=VMEM_LIMIT),
        cost_estimate=pl.CostEstimate(flops=int(flops), bytes_accessed=int(size), transcendentals=0),
        name=name,
    )(*operands)


def full(*shape):
    return jax.ShapeDtypeStruct(shape, F32)


def shards(
    cells,
    w_send,
    w_recv,
    w_msg,
    w_coarse,
    w_self,
    w_agg,
    w_up,
    w_out,
    upstream,
    senders,
    receivers,
    send_map,
    pool_map,
    coarse_senders,
    coarse_receivers,
):
    count, latent = cells.shape
    blocks = lax.axis_size("space")
    place = jnp.stack([lax.axis_index("space"), lax.axis_index("coarse")]).astype(jnp.int32)
    coarse_total = coarse_senders.shape[0] * 2 // 6
    coarse_block = coarse_total // blocks
    rows = 2 * coarse_block
    half = coarse_block // 2
    slots = send_map.shape[2]
    edges = senders.shape[0]
    nodes = 2 * count + 4 * slots
    pool_scale = (coarse_block / count) ** 0.5
    grad_scale = (count * blocks) ** (-0.5)
    sizes = (coarse_block, coarse_total)

    def lanes(array):
        return array.reshape(-1, LANES)

    send_rows, recv_rows = lanes(senders), lanes(receivers)
    map_rows, pool_rows = lanes(send_map), lanes(pool_map)
    coarse_send, coarse_recv = lanes(coarse_senders), lanes(coarse_receivers)

    def other_core(array):
        return lax.ppermute(array, "coarse", [(0, 1), (1, 0)])

    def along(array, by):
        pairs = []
        for block in range(blocks):
            for core, step in ((0, by), (1, -by)):
                if 0 <= block + step < blocks:
                    pairs.append((2 * block + core, 2 * (block + step) + core))
        return lax.ppermute(array, ("space", "coarse"), pairs)

    def around(array, by):
        return lax.ppermute(array, "space", [(i, (i + by) % blocks) for i in range(blocks)])

    def everywhere(array):
        copies = jnp.broadcast_to(array[None], (blocks,) + array.shape)
        return lax.all_to_all(copies.reshape(-1, latent), "space", 0, 0, tiled=True)

    near, far, pool_part = call(
        functools.partial(pack_kernel, sizes + (pool_scale,)),
        [full(slots, latent), full(slots, latent), full(rows, latent)],
        [],
        2 * 2 * 2 * slots * count * 256,
        "pack",
        place,
        cells,
        map_rows,
        pool_rows,
    )
    pooled_own = pool_part[:coarse_block] + around(pool_part[coarse_block:], 1)
    pooled_half = lax.dynamic_slice_in_dim(pooled_own, place[1] * half, half, 0)
    pooled = everywhere(pooled_half)
    near, far = along(near, 1), along(far, 2)
    near_other, far_other = other_core(near), other_core(far)
    edge_both = other_core(jnp.concatenate([coarse_send, coarse_recv], axis=0))
    chunks = coarse_send.shape[0]
    groups = (blocks * half // LANES) * rows
    count_into, count_from = call(
        functools.partial(count_kernel, sizes),
        [full(groups, LANES), full(groups, LANES)],
        [],
        4 * 2 * groups * LANES * 12 * chunks * LANES,
        "count",
        place,
        coarse_send,
        edge_both[:chunks],
        coarse_recv,
        edge_both[chunks:],
    )
    pre, hidden, agg = call(
        edge_kernel,
        [full(edges, latent), full(edges, latent), full(count, latent)],
        [
            pltpu.VMEM((nodes, 2 * latent), BF16),
            pltpu.VMEM((TILE, nodes), BF16),
            pltpu.VMEM((edges, 2 * latent), BF16),
        ],
        2 * 2 * edges * (nodes + count) * 256,
        "edges",
        place,
        cells,
        near,
        near_other,
        far,
        far_other,
        w_send,
        w_recv,
        w_msg,
        send_rows,
        recv_rows,
    )
    agg_other = other_core(agg)
    (sums,) = call(
        functools.partial(coarse_sum_kernel, (coarse_block, blocks)),
        [full(2 * rows, latent)],
        [],
        6 * 2 * rows * blocks * half * latent,
        "coarse_sum",
        place,
        count_into,
        pooled,
    )
    sums_other = other_core(sums)
    square = pltpu.VMEM((2 * latent, 2 * latent), F32)
    d_agg, d_direct, d_coarse, coarse_in, node_grads = call(
        functools.partial(node_kernel, sizes),
        [
            full(count, latent),
            full(count, latent),
            full(rows, latent),
            full(rows, latent),
            full(4, latent, latent),
        ],
        [square, square, square, pltpu.VMEM((rows, 2 * latent), F32)],
        2 * 2 * 11 * count * 256 * 256,
        "nodes",
        place,
        cells,
        agg,
        agg_other,
        sums,
        sums_other,
        upstream,
        pool_rows,
        w_coarse,
        w_self,
        w_agg,
        w_up,
        w_out,
    )
    d_before = around(d_coarse[coarse_block:], 1)
    base, d_in_half, coarse_grad = call(
        functools.partial(coarse_back_kernel, coarse_block),
        [full(coarse_block, latent), full(half, latent), full(latent, latent)],
        [],
        1e6,
        "coarse_back",
        place,
        d_coarse,
        d_before,
        coarse_in,
        w_coarse,
    )
    base_after = around(base, -1)
    d_in = everywhere(d_in_half)
    near_back, near_other_back, far_back, far_other_back, d_cells_own, edge_grads = call(
        edge_back_kernel,
        [full(slots, latent)] * 4 + [full(count, latent), full(3, latent, latent)],
        [
            pltpu.VMEM((count, 2 * latent), BF16),
            pltpu.VMEM((TILE, count), BF16),
            pltpu.VMEM((edges, 2 * latent), BF16),
            pltpu.VMEM((nodes, 2 * latent), BF16),
            square,
        ],
        2 * 2 * edges * (nodes + count) * 256,
        "edges_back",
        place,
        cells,
        near,
        near_other,
        far,
        far_other,
        w_send,
        w_recv,
        w_msg,
        send_rows,
        recv_rows,
        pre,
        hidden,
        d_agg,
    )
    edge_grads = edge_grads + other_core(edge_grads)
    first = place[1] == 0
    mine = jnp.where(
        first, jnp.concatenate([edge_grads, coarse_grad[None]], axis=0), node_grads
    ).reshape(-1, latent)
    pieces = lax.all_to_all(mine, "space", 0, 0, tiled=True)
    reduced = jnp.sum(pieces.reshape(blocks, -1, latent), axis=0) * grad_scale
    own_grads = everywhere(reduced).reshape(-1, latent, latent)
    weight_grads = lax.all_gather(own_grads, "coarse", axis=0, tiled=True)

    near_back = near_back + other_core(near_other_back)
    far_back = far_back + other_core(far_other_back)
    near_back, far_back = along(near_back, -1), along(far_back, -2)
    d_cells_other = other_core(d_cells_own)
    (back_sums,) = call(
        functools.partial(coarse_back_sum_kernel, rows),
        [full(rows, latent)],
        [],
        6 * 2 * rows * blocks * half * latent,
        "coarse_back_sum",
        count_from,
        d_in,
    )
    (d_cells,) = call(
        functools.partial(finish_kernel, sizes + (pool_scale,)),
        [full(count, latent)],
        [],
        2 * 2 * count * 4 * slots * 256,
        "finish",
        place,
        d_direct,
        d_cells_own,
        d_cells_other,
        near_back,
        other_core(near_back),
        far_back,
        other_core(far_back),
        base,
        base_after,
        back_sums,
        other_core(back_sums),
        map_rows,
        pool_rows,
    )
    return d_cells, weight_grads


def solution(mesh):
    in_specs = (
        P("space", None),
        P(),
        P(),
        P(),
        P(),
        P(),
        P(),
        P(),
        P(),
        P("space", None),
        P(("space", "coarse")),
        P(("space", "coarse")),
        P("space", None, None),
        P("space"),
        P("coarse"),
        P("coarse"),
    )
    out_specs = (P("space", None), P())
    return jax.shard_map(shards, mesh=mesh, in_specs=in_specs, out_specs=out_specs, check_vma=False)
```

```python
import functools

import jax
import jax.numpy as jnp
from jax import lax
from jax.experimental import pallas as pl
from jax.experimental.pallas import tpu as pltpu
from jax.sharding import PartitionSpec as P

EPSILON = 1e-05
LANES = 128
TILE = 1024
F32 = jnp.float32
BF16 = jnp.bfloat16


def split(values):
    high = values.astype(BF16)
    low = (values - high.astype(F32)).astype(BF16)
    return jnp.concatenate([high, low], axis=1)


def fold(values):
    return values[:, :LANES] + values[:, LANES:]


def weight_pair(weight):
    pair = split(weight)
    return jnp.concatenate([pair, pair], axis=0)


def weight_pair_t(weight):
    high = weight.astype(BF16)
    low = (weight - high.astype(F32)).astype(BF16)
    stacked = jnp.concatenate([high, low], axis=0)
    return jnp.concatenate([stacked, stacked], axis=1)


def mm(left, right):
    return lax.dot_general(left, right, (((1,), (0,)), ((), ())), preferred_element_type=F32)


def mm_t(left, right):
    return lax.dot_general(left, right, (((1,), (1,)), ((), ())), preferred_element_type=F32)


def tm_m(left, right):
    return lax.dot_general(left, right, (((0,), (0,)), ((), ())), preferred_element_type=F32)


def outer(left_pair, right_pair):
    full = tm_m(left_pair, right_pair)
    return fold(full[:LANES] + full[LANES:])


def as_column(row):
    return jnp.transpose(jnp.broadcast_to(row, (LANES, LANES)))


def one_hot_rows(row, count):
    column = jnp.concatenate([as_column(row).astype(jnp.int16)] * (count // LANES), axis=1)
    place = lax.broadcasted_iota(jnp.int16, (LANES, count), 1)
    return jnp.where(column == place, jnp.ones((), BF16), jnp.zeros((), BF16))


def one_hot_columns(row, first, count):
    wide = jnp.broadcast_to(row - first, (16, LANES)).astype(jnp.int16)
    wide = jnp.concatenate([wide] * (count // 16), axis=0)
    place = lax.broadcasted_iota(jnp.int16, (count, LANES), 0)
    return jnp.where(wide == place, jnp.ones((), BF16), jnp.zeros((), BF16))


def norm_parts(values):
    centered = values - jnp.mean(values, axis=-1, keepdims=True)
    variance = jnp.mean(centered * centered, axis=-1, keepdims=True)
    scale = lax.rsqrt(variance + EPSILON)
    return centered * scale, scale


def norm_back(normed, scale, cotangent):
    shared = cotangent - normed * jnp.mean(cotangent * normed, axis=-1, keepdims=True)
    return scale * (shared - jnp.mean(shared, axis=-1, keepdims=True))


def sigmoid(values):
    return 1.0 / (1.0 + jnp.exp(-values))


def silu_slope(values, gate):
    return gate * (1.0 + values * (1.0 - gate))


def relative_pool(row, place, coarse_block, coarse_total):
    shifted = row - place * coarse_block
    return jnp.where(shifted < 0, shifted + coarse_total, shifted)


def map_row(send_ref, group, core, chunk):
    at = slice(chunk * LANES, (chunk + 1) * LANES)
    first, second = send_ref[0, 2 * group : 2 * group + 1, at], send_ref[0, 2 * group + 1 : 2 * group + 2, at]
    return jnp.where(core == 0, first, second)


def pack_kernel(sizes, place_ref, cells_ref, send_ref, pool_ref, near_ref, far_ref, pool_out):
    coarse_block, coarse_total, scale = sizes
    core = place_ref[1]
    count = cells_ref.shape[0]
    pair = split(cells_ref[...])
    hot = []
    for chunk in range(count // LANES):
        row = relative_pool(pool_ref[chunk : chunk + 1, :], place_ref[0], coarse_block, coarse_total)
        hot.append(one_hot_columns(row, 0, 2 * coarse_block))
    pool_out[...] = fold(mm(jnp.concatenate(hot, axis=1), pair)) * scale
    for group, out in ((0, near_ref), (1, far_ref)):
        for chunk in range(out.shape[0] // LANES):
            row = map_row(send_ref, group, core, chunk)
            out[chunk * LANES : (chunk + 1) * LANES, :] = fold(mm(one_hot_rows(row, count), pair))


def sender_row(row, core, count, slots):
    return jnp.where(row >= count, row ^ (core * slots), row)


def edge_kernel(
    place_ref,
    cells_ref,
    near_ref,
    near_other_ref,
    far_ref,
    far_other_ref,
    w_send_ref,
    w_recv_ref,
    w_msg_ref,
    send_ref,
    recv_ref,
    pre_ref,
    hidden_ref,
    agg_ref,
    table,
    hot,
    normed,
):
    core = place_ref[1]
    count = cells_ref.shape[0]
    slots = near_ref.shape[0]
    nodes = 2 * count + 4 * slots
    edges = pre_ref.shape[0]
    w_send = weight_pair(w_send_ref[...])
    cells_pair = split(cells_ref[...])
    table[:count, :] = split(fold(mm(cells_pair, w_send)))
    for spot, part in enumerate((near_ref, near_other_ref, far_ref, far_other_ref)):
        start = count + spot * slots
        table[start : start + slots, :] = split(fold(mm(split(part[...]), w_send)))
    table[nodes - count :, :] = split(fold(mm(cells_pair, weight_pair(w_recv_ref[...]))))
    w_msg = weight_pair(w_msg_ref[...])
    chunks = TILE // LANES

    def tile(step, carry):
        start = pl.multiple_of(step * TILE, TILE)
        for chunk in range(chunks):
            place = step * chunks + chunk
            row = sender_row(send_ref[pl.ds(place, 1), :], core, count, slots)
            hot[chunk * LANES : (chunk + 1) * LANES, : nodes - count] = one_hot_rows(row, nodes - count)
            row = recv_ref[pl.ds(place, 1), :]
            hot[chunk * LANES : (chunk + 1) * LANES, nodes - count :] = one_hot_rows(row, count)
        pre = fold(mm(hot[...], table[...]))
        pre_ref[pl.ds(start, TILE), :] = pre
        hidden = fold(mm(split(pre * sigmoid(pre)), w_msg))
        hidden_ref[pl.ds(start, TILE), :] = hidden
        normed[pl.ds(start, TILE), :] = split(norm_parts(hidden)[0])
        return carry

    lax.fori_loop(0, edges // TILE, tile, 0)
    part = 512

    def gather_tile(step, carry):
        first = step * part
        across = [
            one_hot_columns(recv_ref[chunk : chunk + 1, :], first, part)
            for chunk in range(edges // LANES)
        ]
        agg_ref[pl.ds(pl.multiple_of(first, part), part), :] = fold(
            mm(jnp.concatenate(across, axis=1), normed[...])
        )
        return carry

    lax.fori_loop(0, count // part, gather_tile, 0)


def count_kernel(
    sizes, into, place_ref, send_ref, send_other_ref, recv_ref, recv_other_ref, *rest
):
    count_ref = rest[-1]
    coarse_block, coarse_total = sizes
    core = place_ref[1]
    rows = 2 * coarse_block
    half = coarse_block // 2
    own = coarse_total // 2
    count_ref[...] = jnp.zeros_like(count_ref)
    groups = count_ref.shape[0]
    chunks = send_ref.shape[0]
    batch = 8

    for senders, receivers, owner in (
        (send_ref, recv_ref, core),
        (send_other_ref, recv_other_ref, 1 - core),
    ):

        def step(index, carry, senders=senders, receivers=receivers, owner=owner):
            first, second = [], []
            for chunk in range(batch):
                place = index * batch + chunk
                sender = senders[pl.ds(place, 1), :]
                receiver = receivers[pl.ds(place, 1), :] + owner * own
                near, distant = (receiver, sender) if into else (sender, receiver)
                near = relative_pool(near, place_ref[0], coarse_block, coarse_total)
                inside = distant & (coarse_block - 1)
                column = (distant // coarse_block) * half + (inside & (half - 1))
                wanted = ((inside // half) == core) & (near < rows)
                first.append(
                    one_hot_columns(jnp.where(wanted, (column // LANES) * rows + near, -1), 0, groups)
                )
                second.append(one_hot_columns(column & (LANES - 1), 0, LANES))
            count_ref[...] += mm_t(jnp.concatenate(first, axis=1), jnp.concatenate(second, axis=1))
            return carry

        lax.fori_loop(0, chunks // batch, step, 0)


def weigh_counts(count_ref, values_ref, rows):
    total = jnp.zeros((rows, LANES), F32)
    for group in range(count_ref.shape[0] // rows):
        total += jnp.dot(
            count_ref[group * rows : (group + 1) * rows, :],
            values_ref[group * LANES : (group + 1) * LANES, :],
            precision=lax.Precision.HIGHEST,
            preferred_element_type=F32,
        )
    return total


def coarse_sum_kernel(sizes, place_ref, count_ref, values_ref, sums_ref):
    coarse_block, blocks = sizes
    rows = 2 * coarse_block
    half = coarse_block // 2
    place, core = place_ref[0], place_ref[1]
    after = lax.rem(place + 1, blocks)
    sums_ref[:rows, :] = weigh_counts(count_ref, values_ref, rows)
    sums_ref[rows:, :] = jnp.zeros((rows, LANES), F32)
    for spot, block in ((0, place), (1, after)):
        own = values_ref[pl.ds(pl.multiple_of(block * half, half), half), :]
        sums_ref[pl.ds(pl.multiple_of(rows + spot * coarse_block + core * half, half), half), :] = own


def coarse_back_sum_kernel(sizes, place_ref, count_ref, packed_ref, sums_ref, values):
    coarse_block, blocks = sizes
    rows = 2 * coarse_block
    half = coarse_block // 2
    packed = packed_ref[...]
    low = lax.broadcasted_iota(jnp.int32, packed[:, :8].shape, 1) < 4
    second = jnp.where(low, packed[:, 16:], packed[:, 8:16])
    second = jnp.concatenate([second[:, 4:], second[:, :4]], axis=1)
    values[...] = jnp.concatenate([packed[:, :8], second], axis=1)
    flat = values[...].reshape(-1, LANES)
    core = place_ref[1]
    spread = lax.broadcasted_iota(jnp.int32, (coarse_block, LANES), 0) // half == core
    own = []
    for block in (place_ref[0], lax.rem(place_ref[0] + 1, blocks)):
        pair = values[block // 2]
        mine = jnp.where(lax.rem(block, 2) == 0, pair[:half], pair[half:])
        own.append(jnp.where(spread, jnp.concatenate([mine, mine], axis=0), 0.0))
    total = jnp.concatenate(own, axis=0)
    total += jnp.zeros((rows, LANES), F32)
    for group in range(count_ref.shape[0] // rows):
        total += jnp.dot(
            count_ref[group * rows : (group + 1) * rows, :],
            flat[group * LANES : (group + 1) * LANES, :],
            precision=lax.Precision.HIGHEST,
            preferred_element_type=F32,
        )
    sums_ref[...] = total


def node_kernel(
    sizes,
    place_ref,
    cells_ref,
    agg_ref,
    agg_other_ref,
    sums_ref,
    sums_other_ref,
    upstream_ref,
    pool_ref,
    w_coarse_ref,
    w_self_ref,
    w_agg_ref,
    w_up_ref,
    w_out_ref,
    d_agg_ref,
    d_direct_ref,
    d_coarse_ref,
    coarse_in_ref,
    grads_ref,
    g_self,
    g_agg,
    g_out,
    lifted_back,
):
    coarse_block, coarse_total = sizes
    rows = 2 * coarse_block
    count = cells_ref.shape[0]
    sums = sums_ref[...] + sums_other_ref[...]
    pooled = sums[rows:]
    coarse_in = pooled + sums[:rows]
    coarse_in_ref[...] = coarse_in
    coarse_pre = fold(mm(split(coarse_in), weight_pair(w_coarse_ref[...])))
    coarse_new = pooled + coarse_pre * sigmoid(coarse_pre)
    raised = fold(mm(split(coarse_new), weight_pair(w_up_ref[...])))
    raised = split(jnp.concatenate([raised, jnp.zeros((LANES - rows, LANES), F32)], axis=0))
    w_self, w_agg, w_out = w_self_ref[...], w_agg_ref[...], w_out_ref[...]
    self_pair, agg_pair, out_pair = weight_pair(w_self), weight_pair(w_agg), weight_pair(w_out)
    self_back, agg_back, out_back = weight_pair_t(w_self), weight_pair_t(w_agg), weight_pair_t(w_out)
    part = 256
    g_self[...] = jnp.zeros_like(g_self)
    g_agg[...] = jnp.zeros_like(g_agg)
    g_out[...] = jnp.zeros_like(g_out)
    lifted_back[...] = jnp.zeros_like(lifted_back)

    def tile(step, carry):
        at = pl.ds(pl.multiple_of(step * part, part), part)
        cells_pair = split(cells_ref[at, :])
        agg_pair_rows = split(agg_ref[at, :] + agg_other_ref[at, :])
        down, across = [], []
        for chunk in range(part // LANES):
            row = pool_ref[pl.ds(step * (part // LANES) + chunk, 1), :]
            row = relative_pool(row, place_ref[0], coarse_block, coarse_total)
            down.append(one_hot_rows(row, LANES))
            across.append(one_hot_columns(row, 0, rows))
        inner = fold(
            mm(cells_pair, self_pair)
            + mm(agg_pair_rows, agg_pair)
            + mm(jnp.concatenate(down, axis=0), raised)
        )
        gate = sigmoid(inner)
        active = split(inner * gate)
        normed, scale = norm_parts(fold(mm(active, out_pair)))
        upstream = upstream_ref[at, :]
        d_hidden = split(norm_back(normed, scale, upstream))
        g_out[...] += tm_m(active, d_hidden)
        d_inner = fold(mm_t(d_hidden, out_back)) * silu_slope(inner, gate)
        d_pair = split(d_inner)
        d_agg_ref[at, :] = fold(mm_t(d_pair, agg_back))
        d_direct_ref[at, :] = upstream + fold(mm_t(d_pair, self_back))
        g_self[...] += tm_m(cells_pair, d_pair)
        g_agg[...] += tm_m(agg_pair_rows, d_pair)
        lifted_back[...] += mm(jnp.concatenate(across, axis=1), d_pair)
        return carry

    lax.fori_loop(0, count // part, tile, 0)

    def combine(full):
        return fold(full[:LANES] + full[LANES:])

    inner_sums = split(fold(lifted_back[...]))
    d_coarse_ref[...] = fold(mm_t(inner_sums, weight_pair_t(w_up_ref[...])))
    grads_ref[0] = combine(g_self[...])
    grads_ref[1] = combine(g_agg[...])
    grads_ref[2] = outer(split(coarse_new), inner_sums)
    grads_ref[3] = combine(g_out[...])


def coarse_back_kernel(
    coarse_block, place_ref, own_ref, before_ref, coarse_in_ref, w_coarse_ref, d_in_ref, g_ref
):
    coarse_in = split(coarse_in_ref[:coarse_block, :])
    weight = w_coarse_ref[...]
    pre = fold(mm(coarse_in, weight_pair(weight)))
    d_coarse = own_ref[:coarse_block, :] + before_ref[...]
    d_pre = split(d_coarse * silu_slope(pre, sigmoid(pre)))
    d_in = fold(mm_t(d_pre, weight_pair_t(weight)))
    d_in_ref[...] = d_in
    g_ref[...] = outer(coarse_in, d_pre)


def assemble_kernel(place_ref, d_in_ref, edge_ref, edge_other_ref, coarse_ref, node_ref, out_ref):
    core = place_ref[1]
    d_in = d_in_ref[pl.ds(pl.multiple_of(core * 8, 8), 8), :]
    turned = jnp.concatenate([d_in[4:], d_in[:4]], axis=0)[None]
    out_ref[:, :8, :] = jnp.broadcast_to(d_in[None], (out_ref.shape[0], 8, LANES))
    low = lax.broadcasted_iota(jnp.int32, (1, 8, LANES), 1) < 4

    def put(spot, grads):
        per = grads.shape[0] // 8
        pairs = grads.reshape(per, 8, LANES)
        at = pl.ds(spot * per, per)
        out_ref[at, 8:16, :] = jnp.where(low, pairs, turned)
        out_ref[at, 16:, :] = jnp.where(low, turned, pairs)

    @pl.when(core == 0)
    def _():
        for spot in range(3):
            put(spot, edge_ref[spot] + edge_other_ref[spot])
        put(3, coarse_ref[...])

    @pl.when(core != 0)
    def _():
        for spot in range(4):
            put(spot, node_ref[spot])


def reduce_kernel(scale, packed_ref, count_ref, near_ref, far_ref, out_ref):
    middle, last = packed_ref[:, 8:16, :], packed_ref[:, 16:, :]
    low = lax.broadcasted_iota(jnp.int32, middle.shape, 1) < 4
    total = jnp.sum(jnp.where(low, middle, last), axis=0) * scale
    total = total + jnp.concatenate([total[4:], total[:4]], axis=0)
    out_ref[...] = jnp.broadcast_to(total[None], out_ref.shape)


def edge_back_kernel(
    w_msg_ref,
    recv_ref,
    pre_ref,
    hidden_ref,
    d_agg_ref,
    d_pre,
    g_ref,
    d_agg,
    hot,
    g_msg,
):
    count = d_agg_ref.shape[0]
    edges = pre_ref.shape[0]
    chunks = TILE // LANES
    d_agg[...] = split(d_agg_ref[...])
    msg_back = weight_pair_t(w_msg_ref[...])
    g_msg[...] = jnp.zeros_like(g_msg)

    def tile(step, carry):
        at = pl.ds(pl.multiple_of(step * TILE, TILE), TILE)
        for chunk in range(chunks):
            row = recv_ref[pl.ds(step * chunks + chunk, 1), :]
            hot[chunk * LANES : (chunk + 1) * LANES, :] = one_hot_rows(row, count)
        normed, scale = norm_parts(hidden_ref[at, :])
        d_hidden = split(norm_back(normed, scale, fold(mm(hot[...], d_agg[...]))))
        pre = pre_ref[at, :]
        gate = sigmoid(pre)
        g_msg[...] += tm_m(split(pre * gate), d_hidden)
        d_pre[at, :] = split(fold(mm_t(d_hidden, msg_back)) * silu_slope(pre, gate))
        return carry

    lax.fori_loop(0, edges // TILE, tile, 0)
    full_sum = g_msg[...]
    g_ref[...] = fold(full_sum[:LANES] + full_sum[LANES:])


def edge_table_kernel(
    place_ref,
    cells_ref,
    near_ref,
    near_other_ref,
    far_ref,
    far_other_ref,
    send_ref,
    recv_ref,
    d_pre,
    g_msg,
    d_in_ref,
    d_after_ref,
    d_table,
    grads_ref,
):
    core = place_ref[1]
    count = cells_ref.shape[0]
    slots = near_ref.shape[0]
    nodes = 2 * count + 4 * slots
    edges = d_pre.shape[0]
    part = 1024

    def scatter_tile(step, carry):
        first = step * part
        own = first < nodes - count
        across = []
        for chunk in range(edges // LANES):
            sender = sender_row(send_ref[chunk : chunk + 1, :], core, count, slots)
            receiver = recv_ref[chunk : chunk + 1, :] + (nodes - count)
            across.append(one_hot_columns(jnp.where(own, sender, receiver), first, part))
        d_table[pl.ds(pl.multiple_of(first, part), part), :] = split(
            fold(mm(jnp.concatenate(across, axis=1), d_pre[...]))
        )
        return carry

    lax.fori_loop(0, nodes // part, scatter_tile, 0)
    cells_pair = split(cells_ref[...])
    g_send = tm_m(cells_pair, d_table[:count, :])
    for spot, part_ref in enumerate((near_ref, near_other_ref, far_ref, far_other_ref)):
        start = count + spot * slots
        g_send += tm_m(split(part_ref[...]), d_table[start : start + slots, :])

    grads_ref[0] = fold(g_send[:LANES] + g_send[LANES:])
    grads_ref[1] = outer(cells_pair, d_table[nodes - count :, :])
    grads_ref[2] = g_msg[...]


def edge_out_kernel(
    d_table,
    w_send_ref,
    w_recv_ref,
    near_back,
    near_other_back,
    far_back,
    far_other_back,
    d_cells_ref,
):
    count = d_cells_ref.shape[0]
    slots = near_back.shape[0]
    send_back = weight_pair_t(w_send_ref[...])
    for spot, back in enumerate((near_back, near_other_back, far_back, far_other_back)):
        start = count + spot * slots
        back[...] = fold(mm_t(d_table[start : start + slots, :], send_back))
    d_cells_ref[...] = fold(
        mm_t(d_table[:count, :], send_back)
        + mm_t(d_table[count + 4 * slots :, :], weight_pair_t(w_recv_ref[...]))
    )


def finish_kernel(
    sizes,
    place_ref,
    direct_ref,
    own_ref,
    other_ref,
    near_ref,
    near_other_ref,
    far_ref,
    far_other_ref,
    d_coarse_ref,
    d_before_ref,
    d_after_ref,
    sums_ref,
    sums_other_ref,
    send_ref,
    pool_ref,
    out_ref,
):
    coarse_block, coarse_total, scale = sizes
    rows = 2 * coarse_block
    core = place_ref[1]
    count = direct_ref.shape[0]
    pooled = jnp.concatenate([d_before_ref[...], d_after_ref[...]], axis=0) + d_coarse_ref[...]
    pooled = (pooled + sums_ref[...] + sums_other_ref[...]) * scale
    pooled = split(jnp.concatenate([pooled, jnp.zeros((LANES - rows, LANES), F32)], axis=0))
    returned = split(
        jnp.concatenate([near_ref[...], near_other_ref[...], far_ref[...], far_other_ref[...]], axis=0)
    )
    per = send_ref.shape[2] // LANES
    part = 512

    def tile(step, carry):
        first = step * part
        at = pl.ds(pl.multiple_of(first, part), part)
        across = []
        for group, place in ((0, core), (0, 1 - core), (1, core), (1, 1 - core)):
            for chunk in range(per):
                row = map_row(send_ref, group, place, chunk)
                across.append(one_hot_columns(row, first, part))
        down = []
        for chunk in range(part // LANES):
            row = pool_ref[pl.ds(step * (part // LANES) + chunk, 1), :]
            row = relative_pool(row, place_ref[0], coarse_block, coarse_total)
            down.append(one_hot_rows(row, LANES))
        added = mm(jnp.concatenate(across, axis=1), returned) + mm(
            jnp.concatenate(down, axis=0), pooled
        )
        out_ref[at, :] = direct_ref[at, :] + own_ref[at, :] + other_ref[at, :] + fold(added)
        return carry

    lax.fori_loop(0, count // part, tile, 0)


def call(kernel, outs, scratch, micros, name, *operands, after=(), limit=16):
    whole = pl.BlockSpec(memory_space=pltpu.VMEM)
    specs = [pl.BlockSpec(memory_space=pltpu.SMEM) if o.ndim == 1 else whole for o in operands]
    specs += [pl.BlockSpec(memory_space=pl.ANY)] * len(after)
    operands = operands + tuple(after)
    flops = micros * 1.1e9
    size = micros * 1e6
    return pl.pallas_call(
        kernel,
        out_shape=outs,
        in_specs=specs,
        out_specs=[whole] * len(outs),
        scratch_shapes=scratch,
        compiler_params=pltpu.CompilerParams(vmem_limit_bytes=limit * 1024 * 1024),
        cost_estimate=pl.CostEstimate(flops=int(flops), bytes_accessed=int(size), transcendentals=0),
        name=name,
    )(*operands)


def full(*shape):
    return jax.ShapeDtypeStruct(shape, F32)


def shards(
    cells,
    w_send,
    w_recv,
    w_msg,
    w_coarse,
    w_self,
    w_agg,
    w_up,
    w_out,
    upstream,
    senders,
    receivers,
    send_map,
    pool_map,
    coarse_senders,
    coarse_receivers,
):
    count, latent = cells.shape
    blocks = lax.axis_size("space")
    place = jnp.stack([lax.axis_index("space"), lax.axis_index("coarse")]).astype(jnp.int32)
    coarse_total = coarse_senders.shape[0] * 2 // 6
    coarse_block = coarse_total // blocks
    rows = 2 * coarse_block
    half = coarse_block // 2
    slots = send_map.shape[2]
    edges = senders.shape[0]
    nodes = 2 * count + 4 * slots
    pool_scale = (coarse_block / count) ** 0.5
    grad_scale = (count * blocks) ** (-0.5)
    sizes = (coarse_block, coarse_total)

    def lanes(array):
        return array.reshape(-1, LANES)

    send_rows, recv_rows = lanes(senders), lanes(receivers)
    pool_rows = lanes(pool_map)
    coarse_send, coarse_recv = lanes(coarse_senders), lanes(coarse_receivers)

    def other_core(array):
        return lax.ppermute(array, "coarse", [(0, 1), (1, 0)])

    def along(array, by):
        pairs = []
        for block in range(blocks):
            for core, step in ((0, by), (1, -by)):
                if 0 <= block + step < blocks:
                    pairs.append((2 * block + core, 2 * (block + step) + core))
        return lax.ppermute(array, ("space", "coarse"), pairs)

    def around(array, by):
        return lax.ppermute(array, "space", [(i, (i + by) % blocks) for i in range(blocks)])

    def exchange(array):
        pieces = array.reshape(-1, 4, latent)
        return lax.all_to_all(pieces, "space", 0, 0, tiled=True).reshape(array.shape)

    edge_both = other_core(jnp.concatenate([coarse_send, coarse_recv], axis=0))
    chunks = coarse_send.shape[0]
    groups = (blocks * half // LANES) * rows
    coarse_edges = (coarse_send, edge_both[:chunks], coarse_recv, edge_both[chunks:])
    near, far, pool_part = call(
        functools.partial(pack_kernel, sizes + (pool_scale,)),
        [full(slots, latent), full(slots, latent), full(rows, latent)],
        [],
        1,
        "pack",
        place,
        cells,
        send_map,
        pool_rows,
    )
    pooled_own = pool_part[:coarse_block] + around(pool_part[coarse_block:], 1)
    pooled_half = lax.dynamic_slice_in_dim(pooled_own, place[1] * half, half, 0)
    copies = jnp.broadcast_to(pooled_half[None], (blocks, half, latent))
    pooled = lax.all_to_all(copies, "space", 0, 0, tiled=True).reshape(-1, latent)
    near, far = along(near, 1), along(far, 2)
    near_other, far_other = other_core(near), other_core(far)
    pre, hidden, agg = call(
        edge_kernel,
        [full(edges, latent), full(edges, latent), full(count, latent)],
        [
            pltpu.VMEM((nodes, 2 * latent), BF16),
            pltpu.VMEM((TILE, nodes), BF16),
            pltpu.VMEM((edges, 2 * latent), BF16),
        ],
        11,
        "edges",
        place,
        cells,
        near,
        near_other,
        far,
        far_other,
        w_send,
        w_recv,
        w_msg,
        send_rows,
        recv_rows,
        limit=20,
    )
    agg_other = other_core(agg)
    (count_into,) = call(
        functools.partial(count_kernel, sizes, True),
        [full(groups, LANES)],
        [],
        4,
        "count_into",
        place,
        *coarse_edges,
        after=(agg,),
    )
    (sums,) = call(
        functools.partial(coarse_sum_kernel, (coarse_block, blocks)),
        [full(2 * rows, latent)],
        [],
        1,
        "coarse_sum",
        place,
        count_into,
        pooled,
    )
    sums_other = other_core(sums)
    square = pltpu.VMEM((2 * latent, 2 * latent), F32)
    d_agg, d_direct, d_coarse, coarse_in, node_grads = call(
        functools.partial(node_kernel, sizes),
        [
            full(count, latent),
            full(count, latent),
            full(rows, latent),
            full(rows, latent),
            full(4, latent, latent),
        ],
        [square, square, square, pltpu.VMEM((rows, 2 * latent), F32)],
        6,
        "nodes",
        place,
        cells,
        agg,
        agg_other,
        sums,
        sums_other,
        upstream,
        pool_rows,
        w_coarse,
        w_self,
        w_agg,
        w_up,
        w_out,
    )
    d_before = around(d_coarse[coarse_block:], 1)
    d_after = around(d_coarse[:coarse_block], -1)
    d_pre, msg_grad = call(
        edge_back_kernel,
        [jax.ShapeDtypeStruct((edges, 2 * latent), BF16), full(latent, latent)],
        [
            pltpu.VMEM((count, 2 * latent), BF16),
            pltpu.VMEM((TILE, count), BF16),
            square,
        ],
        5,
        "edges_back",
        w_msg,
        recv_rows,
        pre,
        hidden,
        d_agg,
    )
    d_in, coarse_grad = call(
        functools.partial(coarse_back_kernel, coarse_block),
        [full(coarse_block, latent), full(latent, latent)],
        [],
        1,
        "coarse_back",
        place,
        d_coarse,
        d_before,
        coarse_in,
        w_coarse,
    )
    d_table, edge_grads = call(
        edge_table_kernel,
        [jax.ShapeDtypeStruct((nodes, 2 * latent), BF16), full(3, latent, latent)],
        [],
        8,
        "edges_table",
        place,
        cells,
        near,
        near_other,
        far,
        far_other,
        send_rows,
        recv_rows,
        d_pre,
        msg_grad,
        after=(d_in, d_after),
    )
    near_back, near_other_back, far_back, far_other_back, d_cells_own = call(
        edge_out_kernel,
        [full(slots, latent)] * 4 + [full(count, latent)],
        [],
        2,
        "edges_out",
        d_table,
        w_send,
        w_recv,
    )
    (packed,) = call(
        assemble_kernel,
        [full(blocks // 2, 24, latent)],
        [],
        1,
        "assemble",
        place,
        d_in,
        edge_grads,
        other_core(edge_grads),
        coarse_grad,
        node_grads,
    )
    near_back = near_back + other_core(near_other_back)
    far_back = far_back + other_core(far_other_back)
    near_back, far_back = along(near_back, -1), along(far_back, -2)
    d_cells_other = other_core(d_cells_own)
    (count_from,) = call(
        functools.partial(count_kernel, sizes, False),
        [full(groups, LANES)],
        [],
        3,
        "count_from",
        place,
        *coarse_edges,
        after=(packed,),
    )
    packed = exchange(packed)
    (copies,) = call(
        functools.partial(reduce_kernel, grad_scale),
        [full(blocks // 2, 8, latent)],
        [],
        1,
        "reduce",
        packed,
        after=(count_from, near_back, far_back),
    )
    own_grads = exchange(copies).reshape(-1, latent, latent)
    weight_grads = lax.all_gather(own_grads, "coarse", axis=0, tiled=True)

    (back_sums,) = call(
        functools.partial(coarse_back_sum_kernel, (coarse_block, blocks)),
        [full(rows, latent)],
        [pltpu.VMEM((blocks // 2, 16, latent), F32)],
        1,
        "coarse_back_sum",
        place,
        count_from,
        packed,
    )
    (d_cells,) = call(
        functools.partial(finish_kernel, sizes + (pool_scale,)),
        [full(count, latent)],
        [],
        3,
        "finish",
        place,
        d_direct,
        d_cells_own,
        d_cells_other,
        near_back,
        other_core(near_back),
        far_back,
        other_core(far_back),
        d_coarse,
        d_before,
        d_after,
        back_sums,
        other_core(back_sums),
        send_map,
        pool_rows,
    )
    return d_cells, weight_grads


def solution(mesh):
    in_specs = (
        P("space", None),
        P(),
        P(),
        P(),
        P(),
        P(),
        P(),
        P(),
        P(),
        P("space", None),
        P(("space", "coarse")),
        P(("space", "coarse")),
        P("space", None, None),
        P("space"),
        P("coarse"),
        P("coarse"),
    )
    out_specs = (P("space", None), P())
    return jax.shard_map(shards, mesh=mesh, in_specs=in_specs, out_specs=out_specs, check_vma=False)
```

```python
import functools

import jax
import jax.numpy as jnp
from jax import lax
from jax.experimental import pallas as pl
from jax.experimental.pallas import tpu as pltpu
from jax.sharding import PartitionSpec as P

EPSILON = 1e-05
LANES = 128
PLANE = ("y", "x")
LINE = ("z",)
SPACE = PLANE + LINE
TILE = 1024
F32 = jnp.float32
BF16 = jnp.bfloat16


def split(values):
    high = values.astype(BF16)
    low = (values - high.astype(F32)).astype(BF16)
    return jnp.concatenate([high, low], axis=1)


def fold(values):
    return values[:, :LANES] + values[:, LANES:]


def weight_pair(weight):
    pair = split(weight)
    return jnp.concatenate([pair, pair], axis=0)


def weight_pair_t(weight):
    high = weight.astype(BF16)
    low = (weight - high.astype(F32)).astype(BF16)
    stacked = jnp.concatenate([high, low], axis=0)
    return jnp.concatenate([stacked, stacked], axis=1)


def mm(left, right):
    return lax.dot_general(left, right, (((1,), (0,)), ((), ())), preferred_element_type=F32)


def mm_t(left, right):
    return lax.dot_general(left, right, (((1,), (1,)), ((), ())), preferred_element_type=F32)


def tm_m(left, right):
    return lax.dot_general(left, right, (((0,), (0,)), ((), ())), preferred_element_type=F32)


def outer(left_pair, right_pair):
    full = tm_m(left_pair, right_pair)
    return fold(full[:LANES] + full[LANES:])


def as_column(row):
    return jnp.transpose(jnp.broadcast_to(row, (LANES, LANES)))


def one_hot_rows(row, count):
    column = jnp.concatenate([as_column(row).astype(jnp.int16)] * (count // LANES), axis=1)
    place = lax.broadcasted_iota(jnp.int16, (LANES, count), 1)
    return jnp.where(column == place, jnp.ones((), BF16), jnp.zeros((), BF16))


def one_hot_columns(row, first, count):
    wide = jnp.broadcast_to(row - first, (16, LANES)).astype(jnp.int16)
    wide = jnp.concatenate([wide] * (count // 16), axis=0)
    place = lax.broadcasted_iota(jnp.int16, (count, LANES), 0)
    return jnp.where(wide == place, jnp.ones((), BF16), jnp.zeros((), BF16))


def norm_parts(values):
    centered = values - jnp.mean(values, axis=-1, keepdims=True)
    variance = jnp.mean(centered * centered, axis=-1, keepdims=True)
    scale = lax.rsqrt(variance + EPSILON)
    return centered * scale, scale


def norm_back(normed, scale, cotangent):
    shared = cotangent - normed * jnp.mean(cotangent * normed, axis=-1, keepdims=True)
    return scale * (shared - jnp.mean(shared, axis=-1, keepdims=True))


def sigmoid(values):
    return 1.0 / (1.0 + jnp.exp(-values))


def silu_slope(values, gate):
    return gate * (1.0 + values * (1.0 - gate))


def relative_pool(row, place, coarse_block, coarse_total):
    shifted = row - place * coarse_block
    return jnp.where(shifted < 0, shifted + coarse_total, shifted)


def own_half(rows, core):
    half = rows.shape[0] // 4
    first = jnp.concatenate([rows[:half], rows[2 * half : 3 * half]], axis=0)
    second = jnp.concatenate([rows[half : 2 * half], rows[3 * half :]], axis=0)
    return jnp.where(core == 0, first, second)


def join_line(parts):
    half = parts.shape[1] // 2
    low, high = parts[:, :half, :], parts[:, half:, :]
    joined = jnp.concatenate([low[:1], low[1:] + high[:-1]], axis=0)
    return jnp.concatenate([joined.reshape(-1, LANES), high[-1]], axis=0)


def join_plane(parts, half):
    body, extra = parts[:, :-half, :], parts[:, -half:, :]
    extra = jnp.concatenate([extra[-1:], extra[:-1]], axis=0)
    body = jnp.concatenate([body[:, :half, :] + extra, body[:, half:, :]], axis=1)
    return body.reshape(-1, LANES)


def map_row(send_ref, group, core, chunk):
    at = slice(chunk * LANES, (chunk + 1) * LANES)
    first, second = send_ref[0, 2 * group : 2 * group + 1, at], send_ref[0, 2 * group + 1 : 2 * group + 2, at]
    return jnp.where(core == 0, first, second)


def pool_kernel(
    sizes, place_ref, cells_hbm, pool_hbm, out_ref, cells, pool, sems
):
    coarse_block, coarse_total, scale = sizes
    loads = [
        pltpu.make_async_copy(cells_hbm, cells, sems.at[0]),
        pltpu.make_async_copy(pool_hbm, pool, sems.at[1]),
    ]
    for load in loads:
        load.start()
    for load in loads:
        load.wait()
    hot = []
    for chunk in range(cells.shape[0] // LANES):
        row = relative_pool(pool[chunk : chunk + 1, :], place_ref[0], coarse_block, coarse_total)
        hot.append(one_hot_columns(row, 0, 2 * coarse_block))
    part = own_half(fold(mm(jnp.concatenate(hot, axis=1), split(cells[...]))) * scale, place_ref[1])
    out_ref[...] = jnp.broadcast_to(part[None], out_ref.shape)


def spread_kernel(parts_ref, count_ref, out_ref):
    rows = join_line(parts_ref[...])
    out_ref[...] = jnp.broadcast_to(rows[None], out_ref.shape)


def halo_kernel(
    place_ref, cells_ref, send_ref, coarse_send_ref, coarse_recv_ref, pool_ref, near_ref, far_ref, edges_ref
):
    core = place_ref[1]
    count = cells_ref.shape[0]
    pair = split(cells_ref[...])
    edges_ref[: coarse_send_ref.shape[0], :] = coarse_send_ref[...]
    edges_ref[coarse_send_ref.shape[0] :, :] = coarse_recv_ref[...]
    for group, out in ((0, near_ref), (1, far_ref)):
        for chunk in range(out.shape[0] // LANES):
            row = map_row(send_ref, group, core, chunk)
            out[chunk * LANES : (chunk + 1) * LANES, :] = fold(mm(one_hot_rows(row, count), pair))


def join_halo_kernel(near_ref, far_ref, spread_ref, out_ref):
    slots = near_ref.shape[0]
    out_ref[:slots, :] = near_ref[...]
    out_ref[slots:, :] = far_ref[...]


def sender_row(row, core, count, slots):
    return jnp.where(row >= count, row ^ (core * slots), row)


def edge_kernel(
    place_ref,
    cells_ref,
    halo_ref,
    halo_other_ref,
    w_send_ref,
    w_recv_ref,
    w_msg_ref,
    send_ref,
    recv_ref,
    pre_hbm,
    agg_ref,
    table,
    hot,
    normed,
    pre_ref,
    sems,
):
    core = place_ref[1]
    count = cells_ref.shape[0]
    slots = halo_ref.shape[0] // 2
    nodes = 2 * count + 4 * slots
    edges = pre_ref.shape[0]
    w_send = weight_pair(w_send_ref[...])
    cells_pair = split(cells_ref[...])
    table[:count, :] = split(fold(mm(cells_pair, w_send)))
    for spot, part in enumerate((halo_ref, halo_other_ref, halo_ref, halo_other_ref)):
        start, at = count + spot * slots, spot // 2 * slots
        table[start : start + slots, :] = split(fold(mm(split(part[at : at + slots, :]), w_send)))
    table[nodes - count :, :] = split(fold(mm(cells_pair, weight_pair(w_recv_ref[...]))))
    w_msg = weight_pair(w_msg_ref[...])
    chunks = TILE // LANES

    def keep(step):
        at = pl.ds(pl.multiple_of(step * TILE, TILE), TILE)
        return pltpu.make_async_copy(pre_ref.at[at], pre_hbm.at[at], sems.at[step])

    def tile(step, carry):
        start = pl.multiple_of(step * TILE, TILE)
        for chunk in range(chunks):
            place = step * chunks + chunk
            row = sender_row(send_ref[pl.ds(place, 1), :], core, count, slots)
            hot[chunk * LANES : (chunk + 1) * LANES, : nodes - count] = one_hot_rows(row, nodes - count)
            row = recv_ref[pl.ds(place, 1), :]
            hot[chunk * LANES : (chunk + 1) * LANES, nodes - count :] = one_hot_rows(row, count)
        pre = fold(mm(hot[...], table[...]))
        pre_ref[pl.ds(start, TILE), :] = pre
        keep(step).start()
        hidden = fold(mm(split(pre * sigmoid(pre)), w_msg))
        normed[pl.ds(start, TILE), :] = split(norm_parts(hidden)[0])
        return carry

    lax.fori_loop(0, edges // TILE, tile, 0)
    part = 512

    def gather_tile(step, carry):
        first = step * part
        across = [
            one_hot_columns(recv_ref[chunk : chunk + 1, :], first, part)
            for chunk in range(edges // LANES)
        ]
        agg_ref[pl.ds(pl.multiple_of(first, part), part), :] = fold(
            mm(jnp.concatenate(across, axis=1), normed[...])
        )
        return carry

    lax.fori_loop(0, count // part, gather_tile, 0)
    for step in range(edges // TILE):
        keep(step).wait()


def count_kernel(
    sizes, into, place_ref, send_ref, send_other_ref, recv_ref, recv_other_ref, *rest
):
    coarse_block, coarse_total = sizes
    count_ref, keys, lows = rest[-3:]
    core = place_ref[1]
    rows = 2 * coarse_block
    half = coarse_block // 2
    own = coarse_total // 2
    groups = count_ref.shape[0]
    chunks = send_ref.shape[0]
    for at, senders, receivers, owner in (
        (0, send_ref, recv_ref, core),
        (chunks, send_other_ref, recv_other_ref, 1 - core),
    ):
        sender, receiver = senders[...], receivers[...] + owner * own
        near, distant = (receiver, sender) if into else (sender, receiver)
        near = relative_pool(near, place_ref[0], coarse_block, coarse_total)
        inside = distant & (coarse_block - 1)
        column = (distant >> (coarse_block.bit_length() - 1)) * half + (inside & (half - 1))
        wanted = (jnp.where(inside >= half, 1, 0) == core) & (near < rows)
        keys[at : at + chunks, :] = jnp.where(
            wanted, (column >> (LANES.bit_length() - 1)) * rows + near, -1
        )
        lows[at : at + chunks, :] = column & (LANES - 1)

    first = [one_hot_columns(keys[at : at + 1, :], 0, groups) for at in range(2 * chunks)]
    second = [one_hot_columns(lows[at : at + 1, :], 0, LANES) for at in range(2 * chunks)]
    count_ref[...] = mm_t(jnp.concatenate(first, axis=1), jnp.concatenate(second, axis=1))


def weigh_counts(count_ref, values_ref, rows):
    total = jnp.zeros((rows, LANES), F32)
    for group in range(count_ref.shape[0] // rows):
        total += jnp.dot(
            count_ref[group * rows : (group + 1) * rows, :],
            values_ref[group * LANES : (group + 1) * LANES, :],
            precision=lax.Precision.HIGHEST,
            preferred_element_type=F32,
        )
    return total


def coarse_sum_kernel(sizes, place_ref, count_ref, parts_ref, sums_ref, values):
    coarse_block, blocks = sizes
    rows = 2 * coarse_block
    half = coarse_block // 2
    place, core = place_ref[0], place_ref[1]
    after = lax.rem(place + 1, blocks)
    values[...] = join_plane(parts_ref[...], half)
    sums_ref[:rows, :] = weigh_counts(count_ref, values, rows)
    sums_ref[rows:, :] = jnp.zeros((rows, LANES), F32)
    for spot, block in ((0, place), (1, after)):
        own = values[pl.ds(pl.multiple_of(block * half, half), half), :]
        sums_ref[pl.ds(pl.multiple_of(rows + spot * coarse_block + core * half, half), half), :] = own


def coarse_back_sum_kernel(sizes, place_ref, count_ref, packed_ref, out_ref, values):
    coarse_block, blocks, share = sizes
    rows = 2 * coarse_block
    half = coarse_block // 2
    place, core = place_ref[0], place_ref[1]
    after = lax.rem(place + 1, blocks)
    plane = packed_ref.shape[0]
    out_ref[: plane * share, :] = packed_ref[:, :share, :].reshape(-1, LANES)
    values[...] = join_plane(packed_ref[:, share:, :], half)
    at = plane * share
    out_ref[at:, :] = weigh_counts(count_ref, values, rows)
    for spot, block in ((0, place), (1, after)):
        own = values[pl.ds(pl.multiple_of(block * half, half), half), :]
        out_ref[pl.ds(pl.multiple_of(at + spot * coarse_block + core * half, half), half), :] += own


def node_kernel(
    sizes,
    place_ref,
    cells_ref,
    agg_ref,
    agg_other_ref,
    sums_ref,
    sums_other_ref,
    upstream_ref,
    pool_ref,
    w_coarse_ref,
    w_self_ref,
    w_agg_ref,
    w_up_ref,
    w_out_ref,
    d_agg_ref,
    d_direct_ref,
    d_coarse_ref,
    g_coarse_ref,
    grads_ref,
    g_self,
    g_agg,
    g_out,
    lifted_back,
):
    coarse_block, coarse_total = sizes
    rows = 2 * coarse_block
    count = cells_ref.shape[0]
    sums = sums_ref[...] + sums_other_ref[...]
    pooled = sums[rows:]
    coarse_in = pooled + sums[:rows]
    coarse_pre = fold(mm(split(coarse_in), weight_pair(w_coarse_ref[...])))
    coarse_gate = sigmoid(coarse_pre)
    coarse_new = pooled + coarse_pre * coarse_gate
    raised = fold(mm(split(coarse_new), weight_pair(w_up_ref[...])))
    raised = split(jnp.concatenate([raised, jnp.zeros((LANES - rows, LANES), F32)], axis=0))
    w_self, w_agg, w_out = w_self_ref[...], w_agg_ref[...], w_out_ref[...]
    self_pair, agg_pair, out_pair = weight_pair(w_self), weight_pair(w_agg), weight_pair(w_out)
    self_back, agg_back, out_back = weight_pair_t(w_self), weight_pair_t(w_agg), weight_pair_t(w_out)
    part = count
    g_self[...] = jnp.zeros_like(g_self)
    g_agg[...] = jnp.zeros_like(g_agg)
    g_out[...] = jnp.zeros_like(g_out)
    lifted_back[...] = jnp.zeros_like(lifted_back)

    def tile(step, carry):
        at = pl.ds(pl.multiple_of(step * part, part), part)
        cells_pair = split(cells_ref[at, :])
        agg_pair_rows = split(agg_ref[at, :] + agg_other_ref[at, :])
        down, across = [], []
        for chunk in range(part // LANES):
            row = pool_ref[pl.ds(step * (part // LANES) + chunk, 1), :]
            row = relative_pool(row, place_ref[0], coarse_block, coarse_total)
            down.append(one_hot_rows(row, LANES))
            across.append(one_hot_columns(row, 0, rows))
        inner = fold(
            mm(cells_pair, self_pair)
            + mm(agg_pair_rows, agg_pair)
            + mm(jnp.concatenate(down, axis=0), raised)
        )
        gate = sigmoid(inner)
        active = split(inner * gate)
        normed, scale = norm_parts(fold(mm(active, out_pair)))
        upstream = upstream_ref[at, :]
        d_hidden = split(norm_back(normed, scale, upstream))
        g_out[...] += tm_m(active, d_hidden)
        d_inner = fold(mm_t(d_hidden, out_back)) * silu_slope(inner, gate)
        d_pair = split(d_inner)
        d_agg_ref[at, :] = fold(mm_t(d_pair, agg_back))
        d_direct_ref[at, :] = upstream + fold(mm_t(d_pair, self_back))
        g_self[...] += tm_m(cells_pair, d_pair)
        g_agg[...] += tm_m(agg_pair_rows, d_pair)
        lifted_back[...] += mm(jnp.concatenate(across, axis=1), d_pair)
        return carry

    lax.fori_loop(0, count // part, tile, 0)

    def combine(full):
        return fold(full[:LANES] + full[LANES:])

    inner_sums = split(fold(lifted_back[...]))
    d_coarse = fold(mm_t(inner_sums, weight_pair_t(w_up_ref[...])))
    d_coarse_ref[:rows, :] = d_coarse
    d_coarse_pre = split(d_coarse * silu_slope(coarse_pre, coarse_gate))
    d_coarse_ref[rows:, :] = fold(mm_t(d_coarse_pre, weight_pair_t(w_coarse_ref[...])))
    g_coarse_ref[...] = outer(split(coarse_in), d_coarse_pre)
    grads_ref[0] = combine(g_self[...])
    grads_ref[1] = combine(g_agg[...])
    grads_ref[2] = outer(split(coarse_new), inner_sums)
    grads_ref[3] = combine(g_out[...])


def line_kernel(
    scale, place_ref, parts_ref, d_coarse_ref, mine_ref, other_ref, count_ref, out_ref, near_ref, far_ref
):
    total = jnp.sum(parts_ref[...], axis=0) * scale
    core = place_ref[1]
    rows = d_coarse_ref.shape[0] // 2
    d_in = own_half(d_coarse_ref[rows:, :], core)
    out_ref[...] = jnp.broadcast_to(jnp.concatenate([total, d_in], axis=0)[None], out_ref.shape)
    slots = far_ref.shape[0]
    near_ref[:slots, :] = mine_ref[:slots, :] + other_ref[:slots, :]
    near_ref[slots:, :] = jnp.where(core == 0, d_coarse_ref[: rows // 2, :], d_coarse_ref[rows // 2 : rows, :])
    far_ref[...] = mine_ref[slots:, :] + other_ref[slots:, :]


def plane_kernel(share, parts_ref, out_ref):
    total = jnp.sum(parts_ref[:, :share, :], axis=0)
    rows = jnp.concatenate([total, join_line(parts_ref[:, share:, :])], axis=0)
    out_ref[...] = jnp.broadcast_to(rows[None], out_ref.shape)


def edge_back_kernel(
    w_msg_ref,
    recv_ref,
    pre_ref,
    d_agg_ref,
    d_pre,
    g_ref,
    d_agg,
    hot,
):
    count = d_agg_ref.shape[0]
    edges = pre_ref.shape[0]
    d_agg[...] = split(d_agg_ref[...])
    for chunk in range(edges // LANES):
        row = recv_ref[chunk : chunk + 1, :]
        hot[chunk * LANES : (chunk + 1) * LANES, :] = one_hot_rows(row, count)
    pre = pre_ref[...]
    gate = sigmoid(pre)
    active = split(pre * gate)
    normed, scale = norm_parts(fold(mm(active, weight_pair(w_msg_ref[...]))))
    d_hidden = split(norm_back(normed, scale, fold(mm(hot[...], d_agg[...]))))
    g_ref[...] = outer(active, d_hidden)
    d_pre[...] = split(fold(mm_t(d_hidden, weight_pair_t(w_msg_ref[...]))) * silu_slope(pre, gate))


def edge_table_kernel(
    place_ref,
    cells_ref,
    halo_ref,
    halo_other_ref,
    w_send_ref,
    w_recv_ref,
    send_ref,
    recv_ref,
    d_pre,
    g_msg,
    direct_ref,
    grads_ref,
    mine_back,
    other_back,
    d_cells_ref,
    d_table,
):
    core = place_ref[1]
    count = cells_ref.shape[0]
    slots = halo_ref.shape[0] // 2
    nodes = 2 * count + 4 * slots
    edges = d_pre.shape[0]
    part = 1024

    def scatter_tile(step, carry):
        first = step * part
        own = first < nodes - count
        across = []
        for chunk in range(edges // LANES):
            sender = sender_row(send_ref[chunk : chunk + 1, :], core, count, slots)
            receiver = recv_ref[chunk : chunk + 1, :] + (nodes - count)
            across.append(one_hot_columns(jnp.where(own, sender, receiver), first, part))
        d_table[pl.ds(pl.multiple_of(first, part), part), :] = split(
            fold(mm(jnp.concatenate(across, axis=1), d_pre[...]))
        )
        return carry

    lax.fori_loop(0, nodes // part, scatter_tile, 0)
    cells_pair = split(cells_ref[...])
    g_send = tm_m(cells_pair, d_table[:count, :])
    for spot, part in enumerate((halo_ref, halo_other_ref, halo_ref, halo_other_ref)):
        start, at = count + spot * slots, spot // 2 * slots
        g_send += tm_m(split(part[at : at + slots, :]), d_table[start : start + slots, :])

    grads_ref[0] = fold(g_send[:LANES] + g_send[LANES:])
    grads_ref[1] = outer(cells_pair, d_table[nodes - count :, :])
    grads_ref[2] = g_msg[...]
    send_back = weight_pair_t(w_send_ref[...])
    for spot, back in enumerate((mine_back, other_back, mine_back, other_back)):
        start = count + spot * slots
        at = spot // 2 * slots
        back[at : at + slots, :] = fold(mm_t(d_table[start : start + slots, :], send_back))
    d_cells = fold(
        mm_t(d_table[:count, :], send_back)
        + mm_t(d_table[nodes - count :, :], weight_pair_t(w_recv_ref[...]))
    )
    d_cells_ref[...] = d_cells + jnp.where(core == 0, direct_ref[...], 0.0)


def gather_back_kernel(sizes, place_ref, own_ref, other_ref, back_ref, back_other_ref, send_ref, out_ref):
    extra, blocks = sizes
    place, core = place_ref[0], place_ref[1]
    count = own_ref.shape[0]
    slots = (back_ref.shape[0] - extra) // 2

    def inside(ref, core):
        edge = jnp.where(core == 0, blocks - 1, 0)
        return jnp.where(place == edge, 0.0, ref[:slots, :])

    returned = split(
        jnp.concatenate(
            [
                inside(back_ref, core),
                inside(back_other_ref, 1 - core),
                back_ref[slots + extra :, :],
                back_other_ref[slots + extra :, :],
            ],
            axis=0,
        )
    )
    part = 512

    def tile(step, carry):
        first = step * part
        at = pl.ds(pl.multiple_of(first, part), part)
        across = []
        for group, place in ((0, core), (0, 1 - core), (1, core), (1, 1 - core)):
            for chunk in range(send_ref.shape[2] // LANES):
                row = map_row(send_ref, group, place, chunk)
                across.append(one_hot_columns(row, first, part))
        added = mm(jnp.concatenate(across, axis=1), returned)
        out_ref[at, :] = own_ref[at, :] + other_ref[at, :] + fold(added)
        return carry

    lax.fori_loop(0, count // part, tile, 0)


def finish_kernel(
    sizes,
    place_ref,
    most_ref,
    d_coarse_ref,
    back_ref,
    back_other_ref,
    mine_ref,
    other_ref,
    pool_ref,
    out_ref,
    grads_ref,
):
    coarse_block, coarse_total, scale = sizes
    rows = 2 * coarse_block
    core = place_ref[1]
    count = most_ref.shape[0]
    weights = mine_ref.shape[0] - rows
    half = grads_ref.shape[0] // 2
    grads_ref[pl.ds(core * half, half)] = mine_ref[:weights, :].reshape(half, LANES, LANES)
    grads_ref[pl.ds((1 - core) * half, half)] = other_ref[:weights, :].reshape(half, LANES, LANES)
    slots = (back_ref.shape[0] - coarse_block) // 2
    at = slice(slots, slots + coarse_block)
    mine, other = back_ref[at, :], back_other_ref[at, :]
    d_before, d_after = jnp.where(core == 0, other, mine), jnp.where(core == 0, mine, other)
    pooled = jnp.concatenate([d_before, d_after], axis=0) + d_coarse_ref[:rows, :]
    pooled = (pooled + mine_ref[weights:, :] + other_ref[weights:, :]) * scale
    pooled = split(jnp.concatenate([pooled, jnp.zeros((LANES - rows, LANES), F32)], axis=0))
    down = []
    for chunk in range(count // LANES):
        row = relative_pool(pool_ref[chunk : chunk + 1, :], place_ref[0], coarse_block, coarse_total)
        down.append(one_hot_rows(row, LANES))
    out_ref[...] = most_ref[...] + fold(mm(jnp.concatenate(down, axis=0), pooled))


MEGABYTES = {
    "pool": 6,
    "halo": 6,
    "count_into": 6,
    "spread": 4,
    "edges": 14,
    "coarse_sum": 4,
    "nodes": 8,
    "edges_back": 14,
    "edges_table": 9,
    "line": 6,
    "plane": 4,
    "gather_back": 8,
    "coarse_back_sum": 6,
    "finish": 6,
    "count_from": 6,
    "join_halo": 4,
}


def call(kernel, outs, scratch, micros, name, *operands, after=(), far=(), far_outs=()):
    whole = pl.BlockSpec(memory_space=pltpu.VMEM)
    outer = pl.BlockSpec(memory_space=pltpu.HBM)
    specs = [pl.BlockSpec(memory_space=pltpu.SMEM) if o.ndim == 1 else whole for o in operands]
    specs = [outer if at in far else spec for at, spec in enumerate(specs)]
    specs += [pl.BlockSpec(memory_space=pl.ANY)] * len(after)
    operands = operands + tuple(after)
    flops = micros * 1.1e9
    size = micros * 1e6
    return pl.pallas_call(
        kernel,
        out_shape=outs,
        in_specs=specs,
        out_specs=[outer if at in far_outs else whole for at in range(len(outs))],
        scratch_shapes=scratch,
        compiler_params=pltpu.CompilerParams(vmem_limit_bytes=MEGABYTES[name] * 1024 * 1024),
        cost_estimate=pl.CostEstimate(flops=int(flops), bytes_accessed=int(size), transcendentals=0),
        name=name,
    )(*operands)


def full(*shape):
    return jax.ShapeDtypeStruct(shape, F32)


def shards(
    cells,
    w_send,
    w_recv,
    w_msg,
    w_coarse,
    w_self,
    w_agg,
    w_up,
    w_out,
    upstream,
    senders,
    receivers,
    send_map,
    pool_map,
    coarse_senders,
    coarse_receivers,
):
    count, latent = cells.shape
    plane, line = lax.axis_size(PLANE), lax.axis_size(LINE)
    blocks = plane * line
    place = jnp.stack([lax.axis_index(SPACE), lax.axis_index("coarse")]).astype(jnp.int32)
    coarse_total = coarse_senders.shape[0] * 2 // 6
    coarse_block = coarse_total // blocks
    rows = 2 * coarse_block
    half = coarse_block // 2
    slots = send_map.shape[2]
    edges = senders.shape[0]
    nodes = 2 * count + 4 * slots
    pool_scale = (coarse_block / count) ** 0.5
    grad_scale = (count * blocks) ** (-0.5)
    sizes = (coarse_block, coarse_total)

    def lanes(array):
        return array.reshape(-1, LANES)

    send_rows, recv_rows = lanes(senders), lanes(receivers)
    pool_rows = lanes(pool_map)
    coarse_send, coarse_recv = lanes(coarse_senders), lanes(coarse_receivers)

    def other_core(array):
        return lax.ppermute(array, "coarse", [(0, 1), (1, 0)])

    def along(array, by, around=False):
        pairs = []
        for block in range(blocks):
            for core, step in ((0, by), (1, -by)):
                if around or 0 <= block + step < blocks:
                    pairs.append((2 * block + core, 2 * ((block + step) % blocks) + core))
        return lax.ppermute(array, SPACE + ("coarse",), pairs)

    def exchange(array, axes):
        return lax.all_to_all(array.reshape(-1, latent), axes, 0, 0, tiled=True)

    chunks = coarse_send.shape[0]
    groups = (blocks * half // LANES) * rows
    edge_keys = pltpu.VMEM((2 * chunks, LANES), jnp.int32)
    (copies,) = call(
        functools.partial(pool_kernel, sizes + (pool_scale,)),
        [full(line, coarse_block, latent)],
        [
            pltpu.VMEM((count, latent), F32),
            pltpu.VMEM((count // LANES, LANES), jnp.int32),
            pltpu.SemaphoreType.DMA((2,)),
        ],
        1,
        "pool",
        place,
        cells,
        pool_rows,
        far=(1, 2),
    )
    parts = exchange(copies, LINE).reshape(line, coarse_block, latent)
    near, far, edge_both = call(
        halo_kernel,
        [
            full(slots, latent),
            full(slots, latent),
            jax.ShapeDtypeStruct((2 * chunks, LANES), jnp.int32),
        ],
        [],
        1,
        "halo",
        place,
        cells,
        send_map,
        coarse_send,
        coarse_recv,
        after=(copies,),
    )
    edge_both = other_core(edge_both)
    coarse_edges = (coarse_send, edge_both[:chunks], coarse_recv, edge_both[chunks:])
    (count_into,) = call(
        functools.partial(count_kernel, sizes, True),
        [full(groups, LANES)],
        [edge_keys, edge_keys],
        3,
        "count_into",
        place,
        *coarse_edges,
    )
    lines = line * half + half
    (copies,) = call(
        spread_kernel,
        [full(plane, lines, latent)],
        [],
        1,
        "spread",
        parts,
        after=(count_into,),
    )
    pooled = exchange(copies, PLANE).reshape(plane, lines, latent)
    (halo,) = call(
        join_halo_kernel,
        [full(2 * slots, latent)],
        [],
        0.5,
        "join_halo",
        along(near, 1),
        along(far, 2),
        after=(copies,),
    )
    halo_other = other_core(halo)
    pre, agg = call(
        edge_kernel,
        [pltpu.HBM((edges, latent), F32), full(count, latent)],
        [
            pltpu.VMEM((nodes, 2 * latent), BF16),
            pltpu.VMEM((TILE, nodes), BF16),
            pltpu.VMEM((edges, 2 * latent), BF16),
            pltpu.VMEM((edges, latent), F32),
            pltpu.SemaphoreType.DMA((edges // TILE,)),
        ],
        3,
        "edges",
        place,
        cells,
        halo,
        halo_other,
        w_send,
        w_recv,
        w_msg,
        send_rows,
        recv_rows,
        far_outs=(0,),
    )
    agg_other = other_core(agg)
    (sums,) = call(
        functools.partial(coarse_sum_kernel, (coarse_block, blocks)),
        [full(2 * rows, latent)],
        [pltpu.VMEM((blocks * half, latent), F32)],
        1,
        "coarse_sum",
        place,
        count_into,
        pooled,
    )
    sums_other = other_core(sums)
    square = pltpu.VMEM((2 * latent, 2 * latent), F32)
    d_agg, d_direct, d_coarse, coarse_grad, node_grads = call(
        functools.partial(node_kernel, sizes),
        [
            full(count, latent),
            full(count, latent),
            full(2 * rows, latent),
            full(latent, latent),
            full(4, latent, latent),
        ],
        [square, square, square, pltpu.VMEM((rows, 2 * latent), F32)],
        6,
        "nodes",
        place,
        cells,
        agg,
        agg_other,
        sums,
        sums_other,
        upstream,
        pool_rows,
        w_coarse,
        w_self,
        w_agg,
        w_up,
        w_out,
    )
    d_pre, msg_grad = call(
        edge_back_kernel,
        [jax.ShapeDtypeStruct((edges, 2 * latent), BF16), full(latent, latent)],
        [
            pltpu.VMEM((count, 2 * latent), BF16),
            pltpu.VMEM((edges, count), BF16),
        ],
        5,
        "edges_back",
        w_msg,
        recv_rows,
        pre,
        d_agg,
    )
    edge_grads, mine_back, other_back, d_cells_own = call(
        edge_table_kernel,
        [
            full(3, latent, latent),
            full(2 * slots, latent),
            full(2 * slots, latent),
            full(count, latent),
        ],
        [pltpu.VMEM((nodes, 2 * latent), BF16)],
        8,
        "edges_table",
        place,
        cells,
        halo,
        halo_other,
        w_send,
        w_recv,
        send_rows,
        recv_rows,
        d_pre,
        msg_grad,
        d_direct,
    )
    edge_grads = edge_grads + other_core(edge_grads)
    mine = jnp.concatenate([edge_grads, coarse_grad[None]], axis=0)
    mine = jnp.where(place[1] == 0, mine, node_grads)
    share = 4 * latent // plane
    parts = exchange(mine, PLANE).reshape(plane, share, latent)
    other_back = other_core(other_back)
    d_cells_other = other_core(d_cells_own)
    (count_from,) = call(
        functools.partial(count_kernel, sizes, False),
        [full(groups, LANES)],
        [edge_keys, edge_keys],
        3,
        "count_from",
        place,
        *coarse_edges,
        after=(mine,),
    )
    copies, near_back, far_back = call(
        functools.partial(line_kernel, grad_scale),
        [
            full(line, share + coarse_block, latent),
            full(slots + coarse_block, latent),
            full(slots, latent),
        ],
        [],
        1,
        "line",
        place,
        parts,
        d_coarse,
        mine_back,
        other_back,
        after=(count_from,),
    )
    back = jnp.concatenate([along(near_back, -1, True), along(far_back, -2)], axis=0)
    back_other = other_core(back)
    parts = exchange(copies, LINE).reshape(line, share + coarse_block, latent)
    (copies,) = call(
        functools.partial(plane_kernel, share),
        [full(plane, share + lines, latent)],
        [],
        1,
        "plane",
        parts,
    )
    packed = exchange(copies, PLANE).reshape(plane, share + lines, latent)
    (most,) = call(
        functools.partial(gather_back_kernel, (coarse_block, blocks)),
        [full(count, latent)],
        [],
        3,
        "gather_back",
        place,
        d_cells_own,
        d_cells_other,
        back,
        back_other,
        send_map,
    )
    (sums,) = call(
        functools.partial(coarse_back_sum_kernel, (coarse_block, blocks, share)),
        [full(4 * latent + rows, latent)],
        [pltpu.VMEM((blocks * half, latent), F32)],
        1,
        "coarse_back_sum",
        place,
        count_from,
        packed,
    )
    return call(
        functools.partial(finish_kernel, sizes + (pool_scale,)),
        [full(count, latent), full(8, latent, latent)],
        [],
        2,
        "finish",
        place,
        most,
        d_coarse,
        back,
        back_other,
        sums,
        other_core(sums),
        pool_rows,
    )


def solution(mesh):
    blocks, cores = mesh.devices.shape
    width = 4
    grid = mesh.devices.reshape(width, width, blocks // (width * width), cores)
    mesh = jax.sharding.Mesh(grid, SPACE + ("coarse",))
    both = SPACE + ("coarse",)
    in_specs = (
        (P(SPACE, None),)
        + (P(),) * 8
        + (P(SPACE, None), P(both), P(both), P(SPACE, None, None), P(SPACE), P("coarse"), P("coarse"))
    )
    out_specs = (P(SPACE, None), P())
    return jax.shard_map(shards, mesh=mesh, in_specs=in_specs, out_specs=out_specs, check_vma=False)
```

```python
import functools

import jax
import jax.numpy as jnp
from jax import lax
from jax.experimental import pallas as pl
from jax.experimental.pallas import tpu as pltpu
from jax.sharding import PartitionSpec as P

EPSILON = 1e-05
LANES = 128
PLANE = ("y", "x")
LINE = ("z",)
SPACE = PLANE + LINE
TILE = 1024
F32 = jnp.float32
BF16 = jnp.bfloat16


def split(values):
    high = values.astype(BF16)
    low = (values - high.astype(F32)).astype(BF16)
    return jnp.concatenate([high, low], axis=1)


def fold(values):
    return values[:, :LANES] + values[:, LANES:]


def weight_pair(weight):
    pair = split(weight)
    return jnp.concatenate([pair, pair], axis=0)


def weight_pair_t(weight):
    high = weight.astype(BF16)
    low = (weight - high.astype(F32)).astype(BF16)
    stacked = jnp.concatenate([high, low], axis=0)
    return jnp.concatenate([stacked, stacked], axis=1)


def mm(left, right):
    return lax.dot_general(left, right, (((1,), (0,)), ((), ())), preferred_element_type=F32)


def mm_t(left, right):
    return lax.dot_general(left, right, (((1,), (1,)), ((), ())), preferred_element_type=F32)


def tm_m(left, right):
    return lax.dot_general(left, right, (((0,), (0,)), ((), ())), preferred_element_type=F32)


def outer(left_pair, right_pair):
    full = tm_m(left_pair, right_pair)
    return fold(full[:LANES] + full[LANES:])


def as_column(row):
    return jnp.transpose(jnp.broadcast_to(row, (LANES, LANES)))


def one_hot_rows(row, count):
    column = jnp.concatenate([as_column(row).astype(jnp.int16)] * (count // LANES), axis=1)
    place = lax.broadcasted_iota(jnp.int16, (LANES, count), 1)
    return jnp.where(column == place, jnp.ones((), BF16), jnp.zeros((), BF16))


def one_hot_columns(row, first, count):
    wide = jnp.broadcast_to(row - first, (16, LANES)).astype(jnp.int16)
    wide = jnp.concatenate([wide] * (count // 16), axis=0)
    place = lax.broadcasted_iota(jnp.int16, (count, LANES), 0)
    return jnp.where(wide == place, jnp.ones((), BF16), jnp.zeros((), BF16))


def norm_parts(values):
    centered = values - jnp.mean(values, axis=-1, keepdims=True)
    variance = jnp.mean(centered * centered, axis=-1, keepdims=True)
    scale = lax.rsqrt(variance + EPSILON)
    return centered * scale, scale


def norm_back(normed, scale, cotangent):
    shared = cotangent - normed * jnp.mean(cotangent * normed, axis=-1, keepdims=True)
    return scale * (shared - jnp.mean(shared, axis=-1, keepdims=True))


def sigmoid(values):
    return 1.0 / (1.0 + jnp.exp(-values))


def silu_slope(values, gate):
    return gate * (1.0 + values * (1.0 - gate))


def relative_pool(row, place, coarse_block, coarse_total):
    shifted = row - place * coarse_block
    return jnp.where(shifted < 0, shifted + coarse_total, shifted)


def own_half(rows, core):
    half = rows.shape[0] // 4
    first = jnp.concatenate([rows[:half], rows[2 * half : 3 * half]], axis=0)
    second = jnp.concatenate([rows[half : 2 * half], rows[3 * half :]], axis=0)
    return jnp.where(core == 0, first, second)


def join_line(parts):
    half = parts.shape[1] // 2
    low, high = parts[:, :half, :], parts[:, half:, :]
    joined = jnp.concatenate([low[:1], low[1:] + high[:-1]], axis=0)
    return jnp.concatenate([joined.reshape(-1, LANES), high[-1]], axis=0)


def join_plane(parts, half):
    body, extra = parts[:, :-half, :], parts[:, -half:, :]
    extra = jnp.concatenate([extra[-1:], extra[:-1]], axis=0)
    body = jnp.concatenate([body[:, :half, :] + extra, body[:, half:, :]], axis=1)
    return body.reshape(-1, LANES)


def map_row(send_ref, group, core, chunk):
    at = slice(chunk * LANES, (chunk + 1) * LANES)
    first, second = send_ref[0, 2 * group : 2 * group + 1, at], send_ref[0, 2 * group + 1 : 2 * group + 2, at]
    return jnp.where(core == 0, first, second)


def pool_kernel(
    sizes, place_ref, cells_hbm, pool_hbm, out_ref, cells, pool, sems
):
    coarse_block, coarse_total, scale = sizes
    loads = [
        pltpu.make_async_copy(cells_hbm, cells, sems.at[0]),
        pltpu.make_async_copy(pool_hbm, pool, sems.at[1]),
    ]
    for load in loads:
        load.start()
    for load in loads:
        load.wait()
    hot = []
    for chunk in range(cells.shape[0] // LANES):
        row = relative_pool(pool[chunk : chunk + 1, :], place_ref[0], coarse_block, coarse_total)
        hot.append(one_hot_columns(row, 0, 2 * coarse_block))
    part = own_half(fold(mm(jnp.concatenate(hot, axis=1), split(cells[...]))) * scale, place_ref[1])
    out_ref[...] = jnp.broadcast_to(part[None], out_ref.shape)


def spread_kernel(parts_ref, count_ref, out_ref):
    rows = join_line(parts_ref[...])
    out_ref[...] = jnp.broadcast_to(rows[None], out_ref.shape)


def halo_kernel(
    place_ref, cells_ref, send_ref, coarse_send_ref, coarse_recv_ref, pool_ref, far_ref, near_ref, edges_ref
):
    core = place_ref[1]
    count = cells_ref.shape[0]
    pair = split(cells_ref[...])
    edges_ref[: coarse_send_ref.shape[0], :] = coarse_send_ref[...]
    edges_ref[coarse_send_ref.shape[0] :, :] = coarse_recv_ref[...]
    for group, out in ((0, near_ref), (1, far_ref)):
        for chunk in range(out.shape[0] // LANES):
            row = map_row(send_ref, group, core, chunk)
            out[chunk * LANES : (chunk + 1) * LANES, :] = fold(mm(one_hot_rows(row, count), pair))


def join_halo_kernel(far_ref, near_ref, spread_ref, out_ref):
    slots = near_ref.shape[0]
    out_ref[:slots, :] = near_ref[...]
    out_ref[slots:, :] = far_ref[...]


def sender_row(row, core, count, slots):
    return jnp.where(row >= count, row ^ (core * slots), row)


def edge_kernel(
    place_ref,
    cells_ref,
    halo_ref,
    halo_other_ref,
    w_send_ref,
    w_recv_ref,
    w_msg_ref,
    send_ref,
    recv_ref,
    pre_hbm,
    agg_ref,
    table,
    hot,
    normed,
    pre_ref,
    sems,
):
    core = place_ref[1]
    count = cells_ref.shape[0]
    slots = halo_ref.shape[0] // 2
    nodes = 2 * count + 4 * slots
    edges = pre_ref.shape[0]
    w_send = weight_pair(w_send_ref[...])
    cells_pair = split(cells_ref[...])
    table[:count, :] = split(fold(mm(cells_pair, w_send)))
    for spot, part in enumerate((halo_ref, halo_other_ref, halo_ref, halo_other_ref)):
        start, at = count + spot * slots, spot // 2 * slots
        table[start : start + slots, :] = split(fold(mm(split(part[at : at + slots, :]), w_send)))
    table[nodes - count :, :] = split(fold(mm(cells_pair, weight_pair(w_recv_ref[...]))))
    w_msg = weight_pair(w_msg_ref[...])
    chunks = TILE // LANES

    def keep(step):
        at = pl.ds(pl.multiple_of(step * TILE, TILE), TILE)
        return pltpu.make_async_copy(pre_ref.at[at], pre_hbm.at[at], sems.at[step])

    def tile(step, carry):
        start = pl.multiple_of(step * TILE, TILE)
        for chunk in range(chunks):
            place = step * chunks + chunk
            row = sender_row(send_ref[pl.ds(place, 1), :], core, count, slots)
            hot[chunk * LANES : (chunk + 1) * LANES, : nodes - count] = one_hot_rows(row, nodes - count)
            row = recv_ref[pl.ds(place, 1), :]
            hot[chunk * LANES : (chunk + 1) * LANES, nodes - count :] = one_hot_rows(row, count)
        pre = fold(mm(hot[...], table[...]))
        pre_ref[pl.ds(start, TILE), :] = pre
        keep(step).start()
        hidden = fold(mm(split(pre * sigmoid(pre)), w_msg))
        normed[pl.ds(start, TILE), :] = split(norm_parts(hidden)[0])
        return carry

    lax.fori_loop(0, edges // TILE, tile, 0)
    part = 512

    def gather_tile(step, carry):
        first = step * part
        across = [
            one_hot_columns(recv_ref[chunk : chunk + 1, :], first, part)
            for chunk in range(edges // LANES)
        ]
        agg_ref[pl.ds(pl.multiple_of(first, part), part), :] = fold(
            mm(jnp.concatenate(across, axis=1), normed[...])
        )
        return carry

    lax.fori_loop(0, count // part, gather_tile, 0)
    for step in range(edges // TILE):
        keep(step).wait()


def count_kernel(
    sizes, into, place_ref, send_ref, send_other_ref, recv_ref, recv_other_ref, *rest
):
    coarse_block, coarse_total = sizes
    count_ref, keys, lows = rest[-3:]
    core = place_ref[1]
    rows = 2 * coarse_block
    half = coarse_block // 2
    own = coarse_total // 2
    groups = count_ref.shape[0]
    chunks = send_ref.shape[0]
    for at, senders, receivers, owner in (
        (0, send_ref, recv_ref, core),
        (chunks, send_other_ref, recv_other_ref, 1 - core),
    ):
        sender, receiver = senders[...], receivers[...] + owner * own
        near, distant = (receiver, sender) if into else (sender, receiver)
        near = relative_pool(near, place_ref[0], coarse_block, coarse_total)
        inside = distant & (coarse_block - 1)
        column = (distant >> (coarse_block.bit_length() - 1)) * half + (inside & (half - 1))
        wanted = (jnp.where(inside >= half, 1, 0) == core) & (near < rows)
        keys[at : at + chunks, :] = jnp.where(
            wanted, (column >> (LANES.bit_length() - 1)) * rows + near, -1
        )
        lows[at : at + chunks, :] = column & (LANES - 1)

    first = [one_hot_columns(keys[at : at + 1, :], 0, groups) for at in range(2 * chunks)]
    second = [one_hot_columns(lows[at : at + 1, :], 0, LANES) for at in range(2 * chunks)]
    count_ref[...] = mm_t(jnp.concatenate(first, axis=1), jnp.concatenate(second, axis=1))


def weigh_counts(count_ref, values_ref, rows):
    total = jnp.zeros((rows, LANES), F32)
    for group in range(count_ref.shape[0] // rows):
        total += jnp.dot(
            count_ref[group * rows : (group + 1) * rows, :],
            values_ref[group * LANES : (group + 1) * LANES, :],
            precision=lax.Precision.HIGHEST,
            preferred_element_type=F32,
        )
    return total


def coarse_sum_kernel(sizes, place_ref, count_ref, parts_ref, sums_ref, values):
    coarse_block, blocks = sizes
    rows = 2 * coarse_block
    half = coarse_block // 2
    place, core = place_ref[0], place_ref[1]
    after = lax.rem(place + 1, blocks)
    values[...] = join_plane(parts_ref[...], half)
    sums_ref[:rows, :] = weigh_counts(count_ref, values, rows)
    sums_ref[rows:, :] = jnp.zeros((rows, LANES), F32)
    for spot, block in ((0, place), (1, after)):
        own = values[pl.ds(pl.multiple_of(block * half, half), half), :]
        sums_ref[pl.ds(pl.multiple_of(rows + spot * coarse_block + core * half, half), half), :] = own


def coarse_back_sum_kernel(sizes, place_ref, count_ref, packed_ref, most_ref, out_ref, values):
    coarse_block, blocks, share = sizes
    rows = 2 * coarse_block
    half = coarse_block // 2
    place, core = place_ref[0], place_ref[1]
    after = lax.rem(place + 1, blocks)
    plane = packed_ref.shape[0]
    out_ref[: plane * share, :] = packed_ref[:, :share, :].reshape(-1, LANES)
    values[...] = join_plane(packed_ref[:, share:, :], half)
    at = plane * share
    out_ref[at:, :] = weigh_counts(count_ref, values, rows)
    for spot, block in ((0, place), (1, after)):
        own = values[pl.ds(pl.multiple_of(block * half, half), half), :]
        out_ref[pl.ds(pl.multiple_of(at + spot * coarse_block + core * half, half), half), :] += own


def node_kernel(
    sizes,
    place_ref,
    cells_ref,
    agg_ref,
    agg_other_ref,
    sums_ref,
    sums_other_ref,
    upstream_ref,
    pool_ref,
    w_coarse_ref,
    w_self_ref,
    w_agg_ref,
    w_up_ref,
    w_out_ref,
    d_agg_ref,
    d_direct_ref,
    d_coarse_ref,
    g_coarse_ref,
    grads_ref,
    g_self,
    g_agg,
    g_out,
    lifted_back,
):
    coarse_block, coarse_total = sizes
    rows = 2 * coarse_block
    count = cells_ref.shape[0]
    sums = sums_ref[...] + sums_other_ref[...]
    pooled = sums[rows:]
    coarse_in = pooled + sums[:rows]
    coarse_pre = fold(mm(split(coarse_in), weight_pair(w_coarse_ref[...])))
    coarse_gate = sigmoid(coarse_pre)
    coarse_new = pooled + coarse_pre * coarse_gate
    raised = fold(mm(split(coarse_new), weight_pair(w_up_ref[...])))
    raised = split(jnp.concatenate([raised, jnp.zeros((LANES - rows, LANES), F32)], axis=0))
    w_self, w_agg, w_out = w_self_ref[...], w_agg_ref[...], w_out_ref[...]
    self_pair, agg_pair, out_pair = weight_pair(w_self), weight_pair(w_agg), weight_pair(w_out)
    self_back, agg_back, out_back = weight_pair_t(w_self), weight_pair_t(w_agg), weight_pair_t(w_out)
    part = count
    g_self[...] = jnp.zeros_like(g_self)
    g_agg[...] = jnp.zeros_like(g_agg)
    g_out[...] = jnp.zeros_like(g_out)
    lifted_back[...] = jnp.zeros_like(lifted_back)

    def tile(step, carry):
        at = pl.ds(pl.multiple_of(step * part, part), part)
        cells_pair = split(cells_ref[at, :])
        agg_pair_rows = split(agg_ref[at, :] + agg_other_ref[at, :])
        down, across = [], []
        for chunk in range(part // LANES):
            row = pool_ref[pl.ds(step * (part // LANES) + chunk, 1), :]
            row = relative_pool(row, place_ref[0], coarse_block, coarse_total)
            down.append(one_hot_rows(row, LANES))
            across.append(one_hot_columns(row, 0, rows))
        inner = fold(
            mm(cells_pair, self_pair)
            + mm(agg_pair_rows, agg_pair)
            + mm(jnp.concatenate(down, axis=0), raised)
        )
        gate = sigmoid(inner)
        active = split(inner * gate)
        normed, scale = norm_parts(fold(mm(active, out_pair)))
        upstream = upstream_ref[at, :]
        d_hidden = split(norm_back(normed, scale, upstream))
        g_out[...] += tm_m(active, d_hidden)
        d_inner = fold(mm_t(d_hidden, out_back)) * silu_slope(inner, gate)
        d_pair = split(d_inner)
        d_agg_ref[at, :] = fold(mm_t(d_pair, agg_back))
        d_direct_ref[at, :] = upstream + fold(mm_t(d_pair, self_back))
        g_self[...] += tm_m(cells_pair, d_pair)
        g_agg[...] += tm_m(agg_pair_rows, d_pair)
        lifted_back[...] += mm(jnp.concatenate(across, axis=1), d_pair)
        return carry

    lax.fori_loop(0, count // part, tile, 0)

    def combine(full):
        return fold(full[:LANES] + full[LANES:])

    inner_sums = split(fold(lifted_back[...]))
    d_coarse = fold(mm_t(inner_sums, weight_pair_t(w_up_ref[...])))
    d_coarse_ref[:rows, :] = d_coarse
    d_coarse_pre = split(d_coarse * silu_slope(coarse_pre, coarse_gate))
    d_coarse_ref[rows:, :] = fold(mm_t(d_coarse_pre, weight_pair_t(w_coarse_ref[...])))
    g_coarse_ref[...] = outer(split(coarse_in), d_coarse_pre)
    grads_ref[0] = combine(g_self[...])
    grads_ref[1] = combine(g_agg[...])
    grads_ref[2] = outer(split(coarse_new), inner_sums)
    grads_ref[3] = combine(g_out[...])


def line_kernel(
    scale, place_ref, parts_ref, d_coarse_ref, mine_ref, other_ref, count_ref, out_ref, far_ref, near_ref
):
    total = jnp.sum(parts_ref[...], axis=0) * scale
    core = place_ref[1]
    rows = d_coarse_ref.shape[0] // 2
    d_in = own_half(d_coarse_ref[rows:, :], core)
    out_ref[...] = jnp.broadcast_to(jnp.concatenate([total, d_in], axis=0)[None], out_ref.shape)
    slots = far_ref.shape[0]
    near_ref[:slots, :] = mine_ref[:slots, :] + other_ref[:slots, :]
    near_ref[slots:, :] = jnp.where(core == 0, d_coarse_ref[: rows // 2, :], d_coarse_ref[rows // 2 : rows, :])
    far_ref[...] = mine_ref[slots:, :] + other_ref[slots:, :]


def plane_kernel(share, parts_ref, out_ref):
    total = jnp.sum(parts_ref[:, :share, :], axis=0)
    rows = jnp.concatenate([total, join_line(parts_ref[:, share:, :])], axis=0)
    out_ref[...] = jnp.broadcast_to(rows[None], out_ref.shape)


def edge_back_kernel(
    w_msg_ref,
    recv_ref,
    pre_ref,
    d_agg_ref,
    d_pre,
    g_ref,
    d_agg,
    hot,
):
    count = d_agg_ref.shape[0]
    edges = pre_ref.shape[0]
    d_agg[...] = split(d_agg_ref[...])
    for chunk in range(edges // LANES):
        row = recv_ref[chunk : chunk + 1, :]
        hot[chunk * LANES : (chunk + 1) * LANES, :] = one_hot_rows(row, count)
    pre = pre_ref[...]
    gate = sigmoid(pre)
    active = split(pre * gate)
    normed, scale = norm_parts(fold(mm(active, weight_pair(w_msg_ref[...]))))
    d_hidden = split(norm_back(normed, scale, fold(mm(hot[...], d_agg[...]))))
    g_ref[...] = outer(active, d_hidden)
    d_pre[...] = split(fold(mm_t(d_hidden, weight_pair_t(w_msg_ref[...]))) * silu_slope(pre, gate))


def edge_table_kernel(
    place_ref,
    cells_ref,
    halo_ref,
    halo_other_ref,
    w_send_ref,
    w_recv_ref,
    send_ref,
    recv_ref,
    d_pre,
    g_msg,
    direct_ref,
    grads_ref,
    mine_back,
    other_back,
    d_cells_ref,
    d_table,
):
    core = place_ref[1]
    count = cells_ref.shape[0]
    slots = halo_ref.shape[0] // 2
    nodes = 2 * count + 4 * slots
    edges = d_pre.shape[0]
    part = 1024

    def scatter_tile(step, carry):
        first = step * part
        own = first < nodes - count
        across = []
        for chunk in range(edges // LANES):
            sender = sender_row(send_ref[chunk : chunk + 1, :], core, count, slots)
            receiver = recv_ref[chunk : chunk + 1, :] + (nodes - count)
            across.append(one_hot_columns(jnp.where(own, sender, receiver), first, part))
        d_table[pl.ds(pl.multiple_of(first, part), part), :] = split(
            fold(mm(jnp.concatenate(across, axis=1), d_pre[...]))
        )
        return carry

    lax.fori_loop(0, nodes // part, scatter_tile, 0)
    cells_pair = split(cells_ref[...])
    g_send = tm_m(cells_pair, d_table[:count, :])
    for spot, part in enumerate((halo_ref, halo_other_ref, halo_ref, halo_other_ref)):
        start, at = count + spot * slots, spot // 2 * slots
        g_send += tm_m(split(part[at : at + slots, :]), d_table[start : start + slots, :])

    grads_ref[0] = fold(g_send[:LANES] + g_send[LANES:])
    grads_ref[1] = outer(cells_pair, d_table[nodes - count :, :])
    grads_ref[2] = g_msg[...]
    send_back = weight_pair_t(w_send_ref[...])
    for spot, back in enumerate((mine_back, other_back, mine_back, other_back)):
        start = count + spot * slots
        at = spot // 2 * slots
        back[at : at + slots, :] = fold(mm_t(d_table[start : start + slots, :], send_back))
    d_cells = fold(
        mm_t(d_table[:count, :], send_back)
        + mm_t(d_table[nodes - count :, :], weight_pair_t(w_recv_ref[...]))
    )
    d_cells_ref[...] = d_cells + jnp.where(core == 0, direct_ref[...], 0.0)


def gather_back_kernel(sizes, place_ref, own_ref, other_ref, back_ref, back_other_ref, send_ref, out_ref):
    extra, blocks = sizes
    place, core = place_ref[0], place_ref[1]
    count = own_ref.shape[0]
    slots = (back_ref.shape[0] - extra) // 2

    def inside(ref, core):
        edge = jnp.where(core == 0, blocks - 1, 0)
        return jnp.where(place == edge, 0.0, ref[:slots, :])

    returned = split(
        jnp.concatenate(
            [
                inside(back_ref, core),
                inside(back_other_ref, 1 - core),
                back_ref[slots + extra :, :],
                back_other_ref[slots + extra :, :],
            ],
            axis=0,
        )
    )
    part = 512

    def tile(step, carry):
        first = step * part
        at = pl.ds(pl.multiple_of(first, part), part)
        across = []
        for group, place in ((0, core), (0, 1 - core), (1, core), (1, 1 - core)):
            for chunk in range(send_ref.shape[2] // LANES):
                row = map_row(send_ref, group, place, chunk)
                across.append(one_hot_columns(row, first, part))
        added = mm(jnp.concatenate(across, axis=1), returned)
        out_ref[at, :] = own_ref[at, :] + other_ref[at, :] + fold(added)
        return carry

    lax.fori_loop(0, count // part, tile, 0)


def finish_kernel(
    sizes,
    place_ref,
    most_ref,
    d_coarse_ref,
    back_ref,
    back_other_ref,
    mine_ref,
    other_ref,
    pool_ref,
    out_ref,
    grads_ref,
):
    coarse_block, coarse_total, scale = sizes
    rows = 2 * coarse_block
    core = place_ref[1]
    count = most_ref.shape[0]
    weights = mine_ref.shape[0] - rows
    half = grads_ref.shape[0] // 2
    grads_ref[pl.ds(core * half, half)] = mine_ref[:weights, :].reshape(half, LANES, LANES)
    grads_ref[pl.ds((1 - core) * half, half)] = other_ref[:weights, :].reshape(half, LANES, LANES)
    slots = (back_ref.shape[0] - coarse_block) // 2
    at = slice(slots, slots + coarse_block)
    mine, other = back_ref[at, :], back_other_ref[at, :]
    d_before, d_after = jnp.where(core == 0, other, mine), jnp.where(core == 0, mine, other)
    pooled = jnp.concatenate([d_before, d_after], axis=0) + d_coarse_ref[:rows, :]
    pooled = (pooled + mine_ref[weights:, :] + other_ref[weights:, :]) * scale
    pooled = split(jnp.concatenate([pooled, jnp.zeros((LANES - rows, LANES), F32)], axis=0))
    down = []
    for chunk in range(count // LANES):
        row = relative_pool(pool_ref[chunk : chunk + 1, :], place_ref[0], coarse_block, coarse_total)
        down.append(one_hot_rows(row, LANES))
    out_ref[...] = most_ref[...] + fold(mm(jnp.concatenate(down, axis=0), pooled))


MEGABYTES = {
    "pool": 6,
    "halo": 6,
    "count_into": 6,
    "spread": 4,
    "edges": 14,
    "coarse_sum": 4,
    "nodes": 8,
    "edges_back": 14,
    "edges_table": 9,
    "line": 6,
    "plane": 4,
    "gather_back": 8,
    "coarse_back_sum": 6,
    "finish": 6,
    "count_from": 6,
    "join_halo": 4,
}


def call(kernel, outs, scratch, micros, name, *operands, after=(), far=(), far_outs=()):
    whole = pl.BlockSpec(memory_space=pltpu.VMEM)
    outer = pl.BlockSpec(memory_space=pltpu.HBM)
    specs = [pl.BlockSpec(memory_space=pltpu.SMEM) if o.ndim == 1 else whole for o in operands]
    specs = [outer if at in far else spec for at, spec in enumerate(specs)]
    specs += [pl.BlockSpec(memory_space=pl.ANY)] * len(after)
    operands = operands + tuple(after)
    flops = micros * 1.1e9
    size = micros * 1e6
    return pl.pallas_call(
        kernel,
        out_shape=outs,
        in_specs=specs,
        out_specs=[outer if at in far_outs else whole for at in range(len(outs))],
        scratch_shapes=scratch,
        compiler_params=pltpu.CompilerParams(vmem_limit_bytes=MEGABYTES[name] * 1024 * 1024),
        cost_estimate=pl.CostEstimate(flops=int(flops), bytes_accessed=int(size), transcendentals=0),
        name=name,
    )(*operands)


def full(*shape):
    return jax.ShapeDtypeStruct(shape, F32)


def shards(
    cells,
    w_send,
    w_recv,
    w_msg,
    w_coarse,
    w_self,
    w_agg,
    w_up,
    w_out,
    upstream,
    senders,
    receivers,
    send_map,
    pool_map,
    coarse_senders,
    coarse_receivers,
):
    count, latent = cells.shape
    plane, line = lax.axis_size(PLANE), lax.axis_size(LINE)
    blocks = plane * line
    place = jnp.stack([lax.axis_index(SPACE), lax.axis_index("coarse")]).astype(jnp.int32)
    coarse_total = coarse_senders.shape[0] * 2 // 6
    coarse_block = coarse_total // blocks
    rows = 2 * coarse_block
    half = coarse_block // 2
    slots = send_map.shape[2]
    edges = senders.shape[0]
    nodes = 2 * count + 4 * slots
    pool_scale = (coarse_block / count) ** 0.5
    grad_scale = (count * blocks) ** (-0.5)
    sizes = (coarse_block, coarse_total)

    def lanes(array):
        return array.reshape(-1, LANES)

    send_rows, recv_rows = lanes(senders), lanes(receivers)
    pool_rows = lanes(pool_map)
    coarse_send, coarse_recv = lanes(coarse_senders), lanes(coarse_receivers)

    def other_core(array):
        return lax.ppermute(array, "coarse", [(0, 1), (1, 0)])

    def along(array, by, around=False):
        pairs = []
        for block in range(blocks):
            for core, step in ((0, by), (1, -by)):
                if around or 0 <= block + step < blocks:
                    pairs.append((2 * block + core, 2 * ((block + step) % blocks) + core))
        return lax.ppermute(array, SPACE + ("coarse",), pairs)

    def exchange(array, axes):
        return lax.all_to_all(array.reshape(-1, latent), axes, 0, 0, tiled=True)

    chunks = coarse_send.shape[0]
    groups = (blocks * half // LANES) * rows
    edge_keys = pltpu.VMEM((2 * chunks, LANES), jnp.int32)
    (copies,) = call(
        functools.partial(pool_kernel, sizes + (pool_scale,)),
        [full(line, coarse_block, latent)],
        [
            pltpu.VMEM((count, latent), F32),
            pltpu.VMEM((count // LANES, LANES), jnp.int32),
            pltpu.SemaphoreType.DMA((2,)),
        ],
        1,
        "pool",
        place,
        cells,
        pool_rows,
        far=(1, 2),
    )
    parts = exchange(copies, LINE).reshape(line, coarse_block, latent)
    far, near, edge_both = call(
        halo_kernel,
        [
            full(slots, latent),
            full(slots, latent),
            jax.ShapeDtypeStruct((2 * chunks, LANES), jnp.int32),
        ],
        [],
        1,
        "halo",
        place,
        cells,
        send_map,
        coarse_send,
        coarse_recv,
        after=(copies,),
    )
    edge_both = other_core(edge_both)
    coarse_edges = (coarse_send, edge_both[:chunks], coarse_recv, edge_both[chunks:])
    (count_into,) = call(
        functools.partial(count_kernel, sizes, True),
        [full(groups, LANES)],
        [edge_keys, edge_keys],
        3,
        "count_into",
        place,
        *coarse_edges,
    )
    lines = line * half + half
    (copies,) = call(
        spread_kernel,
        [full(plane, lines, latent)],
        [],
        1,
        "spread",
        parts,
        after=(count_into,),
    )
    pooled = exchange(copies, PLANE).reshape(plane, lines, latent)
    (halo,) = call(
        join_halo_kernel,
        [full(2 * slots, latent)],
        [],
        0.5,
        "join_halo",
        along(far, 2),
        along(near, 1),
        after=(copies,),
    )
    halo_other = other_core(halo)
    pre, agg = call(
        edge_kernel,
        [pltpu.HBM((edges, latent), F32), full(count, latent)],
        [
            pltpu.VMEM((nodes, 2 * latent), BF16),
            pltpu.VMEM((TILE, nodes), BF16),
            pltpu.VMEM((edges, 2 * latent), BF16),
            pltpu.VMEM((edges, latent), F32),
            pltpu.SemaphoreType.DMA((edges // TILE,)),
        ],
        3,
        "edges",
        place,
        cells,
        halo,
        halo_other,
        w_send,
        w_recv,
        w_msg,
        send_rows,
        recv_rows,
        far_outs=(0,),
    )
    agg_other = other_core(agg)
    (sums,) = call(
        functools.partial(coarse_sum_kernel, (coarse_block, blocks)),
        [full(2 * rows, latent)],
        [pltpu.VMEM((blocks * half, latent), F32)],
        1,
        "coarse_sum",
        place,
        count_into,
        pooled,
    )
    sums_other = other_core(sums)
    square = pltpu.VMEM((2 * latent, 2 * latent), F32)
    d_agg, d_direct, d_coarse, coarse_grad, node_grads = call(
        functools.partial(node_kernel, sizes),
        [
            full(count, latent),
            full(count, latent),
            full(2 * rows, latent),
            full(latent, latent),
            full(4, latent, latent),
        ],
        [square, square, square, pltpu.VMEM((rows, 2 * latent), F32)],
        6,
        "nodes",
        place,
        cells,
        agg,
        agg_other,
        sums,
        sums_other,
        upstream,
        pool_rows,
        w_coarse,
        w_self,
        w_agg,
        w_up,
        w_out,
    )
    d_pre, msg_grad = call(
        edge_back_kernel,
        [jax.ShapeDtypeStruct((edges, 2 * latent), BF16), full(latent, latent)],
        [
            pltpu.VMEM((count, 2 * latent), BF16),
            pltpu.VMEM((edges, count), BF16),
        ],
        5,
        "edges_back",
        w_msg,
        recv_rows,
        pre,
        d_agg,
    )
    edge_grads, mine_back, other_back, d_cells_own = call(
        edge_table_kernel,
        [
            full(3, latent, latent),
            full(2 * slots, latent),
            full(2 * slots, latent),
            full(count, latent),
        ],
        [pltpu.VMEM((nodes, 2 * latent), BF16)],
        8,
        "edges_table",
        place,
        cells,
        halo,
        halo_other,
        w_send,
        w_recv,
        send_rows,
        recv_rows,
        d_pre,
        msg_grad,
        d_direct,
    )
    edge_grads = edge_grads + other_core(edge_grads)
    mine = jnp.concatenate([edge_grads, coarse_grad[None]], axis=0)
    mine = jnp.where(place[1] == 0, mine, node_grads)
    share = 4 * latent // plane
    parts = exchange(mine, PLANE).reshape(plane, share, latent)
    other_back = other_core(other_back)
    d_cells_other = other_core(d_cells_own)
    (count_from,) = call(
        functools.partial(count_kernel, sizes, False),
        [full(groups, LANES)],
        [edge_keys, edge_keys],
        3,
        "count_from",
        place,
        *coarse_edges,
        after=(mine,),
    )
    copies, far_back, near_back = call(
        functools.partial(line_kernel, grad_scale),
        [
            full(line, share + coarse_block, latent),
            full(slots, latent),
            full(slots + coarse_block, latent),
        ],
        [],
        1,
        "line",
        place,
        parts,
        d_coarse,
        mine_back,
        other_back,
        after=(count_from,),
    )
    far_back = along(far_back, -2)
    back = jnp.concatenate([along(near_back, -1, True), far_back], axis=0)
    back_other = other_core(back)
    parts = exchange(copies, LINE).reshape(line, share + coarse_block, latent)
    (copies,) = call(
        functools.partial(plane_kernel, share),
        [full(plane, share + lines, latent)],
        [],
        1,
        "plane",
        parts,
    )
    packed = exchange(copies, PLANE).reshape(plane, share + lines, latent)
    (most,) = call(
        functools.partial(gather_back_kernel, (coarse_block, blocks)),
        [full(count, latent)],
        [],
        3,
        "gather_back",
        place,
        d_cells_own,
        d_cells_other,
        back,
        back_other,
        send_map,
    )
    (sums,) = call(
        functools.partial(coarse_back_sum_kernel, (coarse_block, blocks, share)),
        [full(4 * latent + rows, latent)],
        [pltpu.VMEM((blocks * half, latent), F32)],
        1,
        "coarse_back_sum",
        place,
        count_from,
        packed,
        after=(most,),
    )
    return call(
        functools.partial(finish_kernel, sizes + (pool_scale,)),
        [full(count, latent), full(8, latent, latent)],
        [],
        2,
        "finish",
        place,
        most,
        d_coarse,
        back,
        back_other,
        sums,
        other_core(sums),
        pool_rows,
    )


def solution(mesh):
    blocks, cores = mesh.devices.shape
    width = 4
    grid = mesh.devices.reshape(width, width, blocks // (width * width), cores)
    mesh = jax.sharding.Mesh(grid, SPACE + ("coarse",))
    both = SPACE + ("coarse",)
    in_specs = (
        (P(SPACE, None),)
        + (P(),) * 8
        + (P(SPACE, None), P(both), P(both), P(SPACE, None, None), P(SPACE), P("coarse"), P("coarse"))
    )
    out_specs = (P(SPACE, None), P())
    return jax.shard_map(shards, mesh=mesh, in_specs=in_specs, out_specs=out_specs, check_vma=False)
```

```python
import functools

import jax
import jax.numpy as jnp
from jax import lax
from jax.experimental import pallas as pl
from jax.experimental.pallas import tpu as pltpu
from jax.sharding import PartitionSpec as P

EPSILON = 1e-05
LANES = 128
PLANE = ("y", "x")
LINE = ("z",)
SPACE = PLANE + LINE
TILE = 1024
F32 = jnp.float32
BF16 = jnp.bfloat16


def split(values):
    high = values.astype(BF16)
    low = (values - high.astype(F32)).astype(BF16)
    return jnp.concatenate([high, low], axis=1)


def fold(values):
    return values[:, :LANES] + values[:, LANES:]


def weight_pair(weight):
    pair = split(weight)
    return jnp.concatenate([pair, pair], axis=0)


def weight_pair_t(weight):
    high = weight.astype(BF16)
    low = (weight - high.astype(F32)).astype(BF16)
    stacked = jnp.concatenate([high, low], axis=0)
    return jnp.concatenate([stacked, stacked], axis=1)


def mm(left, right):
    return lax.dot_general(left, right, (((1,), (0,)), ((), ())), preferred_element_type=F32)


def mm_t(left, right):
    return lax.dot_general(left, right, (((1,), (1,)), ((), ())), preferred_element_type=F32)


def tm_m(left, right):
    return lax.dot_general(left, right, (((0,), (0,)), ((), ())), preferred_element_type=F32)


def outer(left_pair, right_pair):
    full = tm_m(left_pair, right_pair)
    return fold(full[:LANES] + full[LANES:])


def as_column(row):
    return jnp.transpose(jnp.broadcast_to(row, (LANES, LANES)))


def one_hot_rows(row, count):
    column = jnp.concatenate([as_column(row).astype(jnp.int16)] * (count // LANES), axis=1)
    place = lax.broadcasted_iota(jnp.int16, (LANES, count), 1)
    return jnp.where(column == place, jnp.ones((), BF16), jnp.zeros((), BF16))


def one_hot_columns(row, first, count):
    wide = jnp.broadcast_to(row - first, (16, LANES)).astype(jnp.int16)
    wide = jnp.concatenate([wide] * (count // 16), axis=0)
    place = lax.broadcasted_iota(jnp.int16, (count, LANES), 0)
    return jnp.where(wide == place, jnp.ones((), BF16), jnp.zeros((), BF16))


def norm_parts(values):
    centered = values - jnp.mean(values, axis=-1, keepdims=True)
    variance = jnp.mean(centered * centered, axis=-1, keepdims=True)
    scale = lax.rsqrt(variance + EPSILON)
    return centered * scale, scale


def norm_back(normed, scale, cotangent):
    shared = cotangent - normed * jnp.mean(cotangent * normed, axis=-1, keepdims=True)
    return scale * (shared - jnp.mean(shared, axis=-1, keepdims=True))


def sigmoid(values):
    return 1.0 / (1.0 + jnp.exp(-values))


def silu_slope(values, gate):
    return gate * (1.0 + values * (1.0 - gate))


def relative_pool(row, place, coarse_block, coarse_total):
    shifted = row - place * coarse_block
    return jnp.where(shifted < 0, shifted + coarse_total, shifted)


def own_half(rows, core):
    half = rows.shape[0] // 4
    first = jnp.concatenate([rows[:half], rows[2 * half : 3 * half]], axis=0)
    second = jnp.concatenate([rows[half : 2 * half], rows[3 * half :]], axis=0)
    return jnp.where(core == 0, first, second)


def join_line(parts):
    half = parts.shape[1] // 2
    low, high = parts[:, :half, :], parts[:, half:, :]
    joined = jnp.concatenate([low[:1], low[1:] + high[:-1]], axis=0)
    return jnp.concatenate([joined.reshape(-1, LANES), high[-1]], axis=0)


def join_plane(parts, half):
    body, extra = parts[:, :-half, :], parts[:, -half:, :]
    extra = jnp.concatenate([extra[-1:], extra[:-1]], axis=0)
    body = jnp.concatenate([body[:, :half, :] + extra, body[:, half:, :]], axis=1)
    return body.reshape(-1, LANES)


def map_row(send_ref, group, core, chunk):
    at = slice(chunk * LANES, (chunk + 1) * LANES)
    first, second = send_ref[0, 2 * group : 2 * group + 1, at], send_ref[0, 2 * group + 1 : 2 * group + 2, at]
    return jnp.where(core == 0, first, second)


def pool_kernel(sizes, place_ref, cells, pool, out_ref):
    coarse_block, scale = sizes
    hot = []
    for chunk in range(cells.shape[0] // LANES):
        hot.append(one_hot_columns(pool[chunk : chunk + 1, :], 0, 2 * coarse_block))
    part = own_half(fold(mm(jnp.concatenate(hot, axis=1), split(cells[...]))) * scale, place_ref[1])
    out_ref[...] = jnp.broadcast_to(part[None], out_ref.shape)


def spread_kernel(parts_ref, count_ref, out_ref):
    rows = join_line(parts_ref[...])
    out_ref[...] = jnp.broadcast_to(rows[None], out_ref.shape)


def halo_kernel(
    place_ref, cells_ref, send_ref, coarse_send_ref, coarse_recv_ref, pool_ref, far_ref, near_ref, edges_ref
):
    core = place_ref[1]
    count = cells_ref.shape[0]
    pair = split(cells_ref[...])
    edges_ref[: coarse_send_ref.shape[0], :] = coarse_send_ref[...]
    edges_ref[coarse_send_ref.shape[0] :, :] = coarse_recv_ref[...]
    for group, out in ((0, near_ref), (1, far_ref)):
        for chunk in range(out.shape[0] // LANES):
            row = map_row(send_ref, group, core, chunk)
            out[chunk * LANES : (chunk + 1) * LANES, :] = fold(mm(one_hot_rows(row, count), pair))


def join_halo_kernel(far_ref, near_ref, spread_ref, out_ref):
    slots = near_ref.shape[0]
    out_ref[:slots, :] = near_ref[...]
    out_ref[slots:, :] = far_ref[...]


def sender_row(row, core, count, slots):
    return jnp.where(row >= count, row ^ (core * slots), row)


def edge_kernel(
    place_ref,
    cells_ref,
    halo_ref,
    halo_other_ref,
    w_send_ref,
    w_recv_ref,
    w_msg_ref,
    send_ref,
    recv_ref,
    pre_hbm,
    agg_ref,
    table,
    hot,
    normed,
    pre_ref,
    sems,
):
    core = place_ref[1]
    count = cells_ref.shape[0]
    slots = halo_ref.shape[0] // 2
    nodes = 2 * count + 4 * slots
    edges = pre_ref.shape[0]
    w_send = weight_pair(w_send_ref[...])
    cells_pair = split(cells_ref[...])
    table[:count, :] = split(fold(mm(cells_pair, w_send)))
    for spot, part in enumerate((halo_ref, halo_other_ref, halo_ref, halo_other_ref)):
        start, at = count + spot * slots, spot // 2 * slots
        table[start : start + slots, :] = split(fold(mm(split(part[at : at + slots, :]), w_send)))
    table[nodes - count :, :] = split(fold(mm(cells_pair, weight_pair(w_recv_ref[...]))))
    w_msg = weight_pair(w_msg_ref[...])
    chunks = TILE // LANES

    def keep(step):
        at = pl.ds(pl.multiple_of(step * TILE, TILE), TILE)
        return pltpu.make_async_copy(pre_ref.at[at], pre_hbm.at[at], sems.at[step])

    def tile(step, carry):
        start = pl.multiple_of(step * TILE, TILE)
        for chunk in range(chunks):
            place = step * chunks + chunk
            row = sender_row(send_ref[pl.ds(place, 1), :], core, count, slots)
            hot[chunk * LANES : (chunk + 1) * LANES, : nodes - count] = one_hot_rows(row, nodes - count)
            row = recv_ref[pl.ds(place, 1), :]
            hot[chunk * LANES : (chunk + 1) * LANES, nodes - count :] = one_hot_rows(row, count)
        pre = fold(mm(hot[...], table[...]))
        pre_ref[pl.ds(start, TILE), :] = pre
        keep(step).start()
        hidden = fold(mm(split(pre * sigmoid(pre)), w_msg))
        normed[pl.ds(start, TILE), :] = split(norm_parts(hidden)[0])
        return carry

    lax.fori_loop(0, edges // TILE, tile, 0)
    part = 512

    def gather_tile(step, carry):
        first = step * part
        across = [
            one_hot_columns(recv_ref[chunk : chunk + 1, :], first, part)
            for chunk in range(edges // LANES)
        ]
        agg_ref[pl.ds(pl.multiple_of(first, part), part), :] = fold(
            mm(jnp.concatenate(across, axis=1), normed[...])
        )
        return carry

    lax.fori_loop(0, count // part, gather_tile, 0)
    for step in range(edges // TILE):
        keep(step).wait()


def count_kernel(
    sizes, into, place_ref, send_ref, send_other_ref, recv_ref, recv_other_ref, *rest
):
    coarse_block, coarse_total = sizes
    count_ref, keys, lows = rest[-3:]
    core = place_ref[1]
    rows = 2 * coarse_block
    half = coarse_block // 2
    own = coarse_total // 2
    groups = count_ref.shape[0]
    chunks = send_ref.shape[0]
    for at, senders, receivers, owner in (
        (0, send_ref, recv_ref, core),
        (chunks, send_other_ref, recv_other_ref, 1 - core),
    ):
        sender, receiver = senders[...], receivers[...] + owner * own
        near, distant = (receiver, sender) if into else (sender, receiver)
        near = relative_pool(near, place_ref[0], coarse_block, coarse_total)
        inside = distant & (coarse_block - 1)
        column = (distant >> (coarse_block.bit_length() - 1)) * half + (inside & (half - 1))
        wanted = (jnp.where(inside >= half, 1, 0) == core) & (near < rows)
        keys[at : at + chunks, :] = jnp.where(
            wanted, (column >> (LANES.bit_length() - 1)) * rows + near, -1
        )
        lows[at : at + chunks, :] = column & (LANES - 1)

    first = [one_hot_columns(keys[at : at + 1, :], 0, groups) for at in range(2 * chunks)]
    second = [one_hot_columns(lows[at : at + 1, :], 0, LANES) for at in range(2 * chunks)]
    count_ref[...] = mm_t(jnp.concatenate(first, axis=1), jnp.concatenate(second, axis=1))


def weigh_counts(count_ref, values_ref, rows):
    total = jnp.zeros((rows, LANES), F32)
    for group in range(count_ref.shape[0] // rows):
        total += jnp.dot(
            count_ref[group * rows : (group + 1) * rows, :],
            values_ref[group * LANES : (group + 1) * LANES, :],
            precision=lax.Precision.HIGHEST,
            preferred_element_type=F32,
        )
    return total


def coarse_sum_kernel(sizes, place_ref, count_ref, parts_ref, sums_ref, values):
    coarse_block, blocks = sizes
    rows = 2 * coarse_block
    half = coarse_block // 2
    place, core = place_ref[0], place_ref[1]
    after = lax.rem(place + 1, blocks)
    values[...] = join_plane(parts_ref[...], half)
    sums_ref[:rows, :] = weigh_counts(count_ref, values, rows)
    sums_ref[rows:, :] = jnp.zeros((rows, LANES), F32)
    for spot, block in ((0, place), (1, after)):
        own = values[pl.ds(pl.multiple_of(block * half, half), half), :]
        sums_ref[pl.ds(pl.multiple_of(rows + spot * coarse_block + core * half, half), half), :] = own


def coarse_back_sum_kernel(sizes, place_ref, count_ref, packed_ref, most_ref, out_ref, values):
    coarse_block, blocks, share = sizes
    rows = 2 * coarse_block
    half = coarse_block // 2
    place, core = place_ref[0], place_ref[1]
    after = lax.rem(place + 1, blocks)
    plane = packed_ref.shape[0]
    out_ref[: plane * share, :] = packed_ref[:, :share, :].reshape(-1, LANES)
    values[...] = join_plane(packed_ref[:, share:, :], half)
    at = plane * share
    out_ref[at:, :] = weigh_counts(count_ref, values, rows)
    for spot, block in ((0, place), (1, after)):
        own = values[pl.ds(pl.multiple_of(block * half, half), half), :]
        out_ref[pl.ds(pl.multiple_of(at + spot * coarse_block + core * half, half), half), :] += own


def node_kernel(
    sizes,
    place_ref,
    cells_ref,
    agg_ref,
    agg_other_ref,
    sums_ref,
    sums_other_ref,
    upstream_ref,
    pool_ref,
    w_coarse_ref,
    w_self_ref,
    w_agg_ref,
    w_up_ref,
    w_out_ref,
    d_agg_ref,
    d_direct_ref,
    d_coarse_ref,
    g_coarse_ref,
    grads_ref,
    g_self,
    g_agg,
    g_out,
    lifted_back,
):
    coarse_block, coarse_total = sizes
    rows = 2 * coarse_block
    count = cells_ref.shape[0]
    sums = sums_ref[...] + sums_other_ref[...]
    pooled = sums[rows:]
    coarse_in = pooled + sums[:rows]
    coarse_pre = fold(mm(split(coarse_in), weight_pair(w_coarse_ref[...])))
    coarse_gate = sigmoid(coarse_pre)
    coarse_new = pooled + coarse_pre * coarse_gate
    raised = fold(mm(split(coarse_new), weight_pair(w_up_ref[...])))
    raised = split(jnp.concatenate([raised, jnp.zeros((LANES - rows, LANES), F32)], axis=0))
    w_self, w_agg, w_out = w_self_ref[...], w_agg_ref[...], w_out_ref[...]
    self_pair, agg_pair, out_pair = weight_pair(w_self), weight_pair(w_agg), weight_pair(w_out)
    self_back, agg_back, out_back = weight_pair_t(w_self), weight_pair_t(w_agg), weight_pair_t(w_out)
    part = count
    g_self[...] = jnp.zeros_like(g_self)
    g_agg[...] = jnp.zeros_like(g_agg)
    g_out[...] = jnp.zeros_like(g_out)
    lifted_back[...] = jnp.zeros_like(lifted_back)

    def tile(step, carry):
        at = pl.ds(pl.multiple_of(step * part, part), part)
        cells_pair = split(cells_ref[at, :])
        agg_pair_rows = split(agg_ref[at, :] + agg_other_ref[at, :])
        down, across = [], []
        for chunk in range(part // LANES):
            row = pool_ref[pl.ds(step * (part // LANES) + chunk, 1), :]
            down.append(one_hot_rows(row, LANES))
            across.append(one_hot_columns(row, 0, rows))
        inner = fold(
            mm(cells_pair, self_pair)
            + mm(agg_pair_rows, agg_pair)
            + mm(jnp.concatenate(down, axis=0), raised)
        )
        gate = sigmoid(inner)
        active = split(inner * gate)
        normed, scale = norm_parts(fold(mm(active, out_pair)))
        upstream = upstream_ref[at, :]
        d_hidden = split(norm_back(normed, scale, upstream))
        g_out[...] += tm_m(active, d_hidden)
        d_inner = fold(mm_t(d_hidden, out_back)) * silu_slope(inner, gate)
        d_pair = split(d_inner)
        d_agg_ref[at, :] = fold(mm_t(d_pair, agg_back))
        d_direct_ref[at, :] = upstream + fold(mm_t(d_pair, self_back))
        g_self[...] += tm_m(cells_pair, d_pair)
        g_agg[...] += tm_m(agg_pair_rows, d_pair)
        lifted_back[...] += mm(jnp.concatenate(across, axis=1), d_pair)
        return carry

    lax.fori_loop(0, count // part, tile, 0)

    def combine(full):
        return fold(full[:LANES] + full[LANES:])

    inner_sums = split(fold(lifted_back[...]))
    d_coarse = fold(mm_t(inner_sums, weight_pair_t(w_up_ref[...])))
    d_coarse_ref[:rows, :] = d_coarse
    d_coarse_pre = split(d_coarse * silu_slope(coarse_pre, coarse_gate))
    d_coarse_ref[rows:, :] = fold(mm_t(d_coarse_pre, weight_pair_t(w_coarse_ref[...])))
    g_coarse_ref[...] = outer(split(coarse_in), d_coarse_pre)
    grads_ref[0] = combine(g_self[...])
    grads_ref[1] = combine(g_agg[...])
    grads_ref[2] = outer(split(coarse_new), inner_sums)
    grads_ref[3] = combine(g_out[...])


def line_kernel(
    scale, place_ref, parts_ref, d_coarse_ref, mine_ref, other_ref, count_ref, out_ref, far_ref, near_ref
):
    total = jnp.sum(parts_ref[...], axis=0) * scale
    core = place_ref[1]
    rows = d_coarse_ref.shape[0] // 2
    d_in = own_half(d_coarse_ref[rows:, :], core)
    out_ref[...] = jnp.broadcast_to(jnp.concatenate([total, d_in], axis=0)[None], out_ref.shape)
    slots = far_ref.shape[0]
    near_ref[:slots, :] = mine_ref[:slots, :] + other_ref[:slots, :]
    near_ref[slots:, :] = jnp.where(core == 0, d_coarse_ref[: rows // 2, :], d_coarse_ref[rows // 2 : rows, :])
    far_ref[...] = mine_ref[slots:, :] + other_ref[slots:, :]


def plane_kernel(share, parts_ref, out_ref):
    total = jnp.sum(parts_ref[:, :share, :], axis=0)
    rows = jnp.concatenate([total, join_line(parts_ref[:, share:, :])], axis=0)
    out_ref[...] = jnp.broadcast_to(rows[None], out_ref.shape)


def edge_back_kernel(
    w_msg_ref,
    recv_ref,
    pre_ref,
    d_agg_ref,
    d_pre,
    g_ref,
    d_agg,
    hot,
):
    count = d_agg_ref.shape[0]
    edges = pre_ref.shape[0]
    d_agg[...] = split(d_agg_ref[...])
    for chunk in range(edges // LANES):
        row = recv_ref[chunk : chunk + 1, :]
        hot[chunk * LANES : (chunk + 1) * LANES, :] = one_hot_rows(row, count)
    pre = pre_ref[...]
    gate = sigmoid(pre)
    active = split(pre * gate)
    normed, scale = norm_parts(fold(mm(active, weight_pair(w_msg_ref[...]))))
    d_hidden = split(norm_back(normed, scale, fold(mm(hot[...], d_agg[...]))))
    g_ref[...] = outer(active, d_hidden)
    d_pre[...] = split(fold(mm_t(d_hidden, weight_pair_t(w_msg_ref[...]))) * silu_slope(pre, gate))


def edge_table_kernel(
    place_ref,
    cells_ref,
    halo_ref,
    halo_other_ref,
    w_send_ref,
    w_recv_ref,
    send_ref,
    recv_ref,
    d_pre,
    g_msg,
    direct_ref,
    grads_ref,
    mine_back,
    other_back,
    d_cells_ref,
    d_table,
):
    core = place_ref[1]
    count = cells_ref.shape[0]
    slots = halo_ref.shape[0] // 2
    nodes = 2 * count + 4 * slots
    edges = d_pre.shape[0]
    part = 1024

    def scatter_tile(step, carry):
        first = step * part
        own = first < nodes - count
        across = []
        for chunk in range(edges // LANES):
            sender = sender_row(send_ref[chunk : chunk + 1, :], core, count, slots)
            receiver = recv_ref[chunk : chunk + 1, :] + (nodes - count)
            across.append(one_hot_columns(jnp.where(own, sender, receiver), first, part))
        d_table[pl.ds(pl.multiple_of(first, part), part), :] = split(
            fold(mm(jnp.concatenate(across, axis=1), d_pre[...]))
        )
        return carry

    lax.fori_loop(0, nodes // part, scatter_tile, 0)
    cells_pair = split(cells_ref[...])
    g_send = tm_m(cells_pair, d_table[:count, :])
    for spot, part in enumerate((halo_ref, halo_other_ref, halo_ref, halo_other_ref)):
        start, at = count + spot * slots, spot // 2 * slots
        g_send += tm_m(split(part[at : at + slots, :]), d_table[start : start + slots, :])

    grads_ref[0] = fold(g_send[:LANES] + g_send[LANES:])
    grads_ref[1] = outer(cells_pair, d_table[nodes - count :, :])
    grads_ref[2] = g_msg[...]
    send_back = weight_pair_t(w_send_ref[...])
    for spot, back in enumerate((mine_back, other_back, mine_back, other_back)):
        start = count + spot * slots
        at = spot // 2 * slots
        back[at : at + slots, :] = fold(mm_t(d_table[start : start + slots, :], send_back))
    d_cells = fold(
        mm_t(d_table[:count, :], send_back)
        + mm_t(d_table[nodes - count :, :], weight_pair_t(w_recv_ref[...]))
    )
    d_cells_ref[...] = d_cells + jnp.where(core == 0, direct_ref[...], 0.0)


def gather_back_kernel(sizes, place_ref, own_ref, other_ref, back_ref, back_other_ref, send_ref, out_ref):
    extra, blocks = sizes
    place, core = place_ref[0], place_ref[1]
    count = own_ref.shape[0]
    slots = (back_ref.shape[0] - extra) // 2

    def inside(ref, core):
        edge = jnp.where(core == 0, blocks - 1, 0)
        return jnp.where(place == edge, 0.0, ref[:slots, :])

    returned = split(
        jnp.concatenate(
            [
                inside(back_ref, core),
                inside(back_other_ref, 1 - core),
                back_ref[slots + extra :, :],
                back_other_ref[slots + extra :, :],
            ],
            axis=0,
        )
    )
    part = 512

    def tile(step, carry):
        first = step * part
        at = pl.ds(pl.multiple_of(first, part), part)
        across = []
        for group, place in ((0, core), (0, 1 - core), (1, core), (1, 1 - core)):
            for chunk in range(send_ref.shape[2] // LANES):
                row = map_row(send_ref, group, place, chunk)
                across.append(one_hot_columns(row, first, part))
        added = mm(jnp.concatenate(across, axis=1), returned)
        out_ref[at, :] = own_ref[at, :] + other_ref[at, :] + fold(added)
        return carry

    lax.fori_loop(0, count // part, tile, 0)


def finish_kernel(
    sizes,
    place_ref,
    most_ref,
    d_coarse_ref,
    back_ref,
    back_other_ref,
    mine_ref,
    other_ref,
    pool_ref,
    out_ref,
    grads_ref,
):
    coarse_block, coarse_total, scale = sizes
    rows = 2 * coarse_block
    core = place_ref[1]
    count = most_ref.shape[0]
    weights = mine_ref.shape[0] - rows
    half = grads_ref.shape[0] // 2
    grads_ref[pl.ds(core * half, half)] = mine_ref[:weights, :].reshape(half, LANES, LANES)
    grads_ref[pl.ds((1 - core) * half, half)] = other_ref[:weights, :].reshape(half, LANES, LANES)
    slots = (back_ref.shape[0] - coarse_block) // 2
    at = slice(slots, slots + coarse_block)
    mine, other = back_ref[at, :], back_other_ref[at, :]
    d_before, d_after = jnp.where(core == 0, other, mine), jnp.where(core == 0, mine, other)
    pooled = jnp.concatenate([d_before, d_after], axis=0) + d_coarse_ref[:rows, :]
    pooled = (pooled + mine_ref[weights:, :] + other_ref[weights:, :]) * scale
    pooled = split(jnp.concatenate([pooled, jnp.zeros((LANES - rows, LANES), F32)], axis=0))
    down = []
    for chunk in range(count // LANES):
        row = pool_ref[chunk : chunk + 1, :]
        down.append(one_hot_rows(row, LANES))
    out_ref[...] = most_ref[...] + fold(mm(jnp.concatenate(down, axis=0), pooled))


MEGABYTES = {
    "pool": 6,
    "halo": 6,
    "count_into": 6,
    "spread": 4,
    "edges": 14,
    "coarse_sum": 4,
    "nodes": 8,
    "edges_back": 14,
    "edges_table": 9,
    "line": 6,
    "plane": 4,
    "gather_back": 8,
    "coarse_back_sum": 6,
    "finish": 6,
    "count_from": 6,
    "join_halo": 4,
}


def call(kernel, outs, scratch, micros, name, *operands, after=(), far=(), far_outs=()):
    whole = pl.BlockSpec(memory_space=pltpu.VMEM)
    outer = pl.BlockSpec(memory_space=pltpu.HBM)
    specs = [pl.BlockSpec(memory_space=pltpu.SMEM) if o.ndim == 1 else whole for o in operands]
    specs = [outer if at in far else spec for at, spec in enumerate(specs)]
    specs += [pl.BlockSpec(memory_space=pl.ANY)] * len(after)
    operands = operands + tuple(after)
    flops = micros * 1.1e9
    size = micros * 1e6
    return pl.pallas_call(
        kernel,
        out_shape=outs,
        in_specs=specs,
        out_specs=[outer if at in far_outs else whole for at in range(len(outs))],
        scratch_shapes=scratch,
        compiler_params=pltpu.CompilerParams(vmem_limit_bytes=MEGABYTES[name] * 1024 * 1024),
        cost_estimate=pl.CostEstimate(flops=int(flops), bytes_accessed=int(size), transcendentals=0),
        name=name,
    )(*operands)


def full(*shape):
    return jax.ShapeDtypeStruct(shape, F32)


def shards(
    cells,
    w_send,
    w_recv,
    w_msg,
    w_coarse,
    w_self,
    w_agg,
    w_up,
    w_out,
    upstream,
    senders,
    receivers,
    send_map,
    pool_map,
    coarse_senders,
    coarse_receivers,
):
    count, latent = cells.shape
    plane, line = lax.axis_size(PLANE), lax.axis_size(LINE)
    blocks = plane * line
    place = jnp.stack([lax.axis_index(SPACE), lax.axis_index("coarse")]).astype(jnp.int32)
    coarse_total = coarse_senders.shape[0] * 2 // 6
    coarse_block = coarse_total // blocks
    rows = 2 * coarse_block
    half = coarse_block // 2
    slots = send_map.shape[2]
    edges = senders.shape[0]
    nodes = 2 * count + 4 * slots
    pool_scale = (coarse_block / count) ** 0.5
    grad_scale = (count * blocks) ** (-0.5)
    sizes = (coarse_block, coarse_total)

    def lanes(array):
        return array.reshape(-1, LANES)

    send_rows, recv_rows = lanes(senders), lanes(receivers)
    pool_rows = lanes(relative_pool(pool_map, place[0], coarse_block, coarse_total))
    coarse_send, coarse_recv = lanes(coarse_senders), lanes(coarse_receivers)

    def other_core(array):
        return lax.ppermute(array, "coarse", [(0, 1), (1, 0)])

    def along(array, by, around=False):
        pairs = []
        for block in range(blocks):
            for core, step in ((0, by), (1, -by)):
                if around or 0 <= block + step < blocks:
                    pairs.append((2 * block + core, 2 * ((block + step) % blocks) + core))
        return lax.ppermute(array, SPACE + ("coarse",), pairs)

    def exchange(array, axes):
        return lax.all_to_all(array.reshape(-1, latent), axes, 0, 0, tiled=True)

    chunks = coarse_send.shape[0]
    groups = (blocks * half // LANES) * rows
    edge_keys = pltpu.VMEM((2 * chunks, LANES), jnp.int32)
    (copies,) = call(
        functools.partial(pool_kernel, (coarse_block, pool_scale)),
        [full(line, coarse_block, latent)],
        [],
        1,
        "pool",
        place,
        cells,
        pool_rows,
    )
    parts = exchange(copies, LINE).reshape(line, coarse_block, latent)
    far, near, edge_both = call(
        halo_kernel,
        [
            full(slots, latent),
            full(slots, latent),
            jax.ShapeDtypeStruct((2 * chunks, LANES), jnp.int32),
        ],
        [],
        1,
        "halo",
        place,
        cells,
        send_map,
        coarse_send,
        coarse_recv,
        after=(copies,),
    )
    edge_both = other_core(edge_both)
    coarse_edges = (coarse_send, edge_both[:chunks], coarse_recv, edge_both[chunks:])
    (count_into,) = call(
        functools.partial(count_kernel, sizes, True),
        [full(groups, LANES)],
        [edge_keys, edge_keys],
        3,
        "count_into",
        place,
        *coarse_edges,
    )
    lines = line * half + half
    (copies,) = call(
        spread_kernel,
        [full(plane, lines, latent)],
        [],
        1,
        "spread",
        parts,
        after=(count_into,),
    )
    pooled = exchange(copies, PLANE).reshape(plane, lines, latent)
    (halo,) = call(
        join_halo_kernel,
        [full(2 * slots, latent)],
        [],
        0.5,
        "join_halo",
        along(far, 2),
        along(near, 1),
        after=(copies,),
    )
    halo_other = other_core(halo)
    pre, agg = call(
        edge_kernel,
        [pltpu.HBM((edges, latent), F32), full(count, latent)],
        [
            pltpu.VMEM((nodes, 2 * latent), BF16),
            pltpu.VMEM((TILE, nodes), BF16),
            pltpu.VMEM((edges, 2 * latent), BF16),
            pltpu.VMEM((edges, latent), F32),
            pltpu.SemaphoreType.DMA((edges // TILE,)),
        ],
        3,
        "edges",
        place,
        cells,
        halo,
        halo_other,
        w_send,
        w_recv,
        w_msg,
        send_rows,
        recv_rows,
        far_outs=(0,),
    )
    agg_other = other_core(agg)
    (sums,) = call(
        functools.partial(coarse_sum_kernel, (coarse_block, blocks)),
        [full(2 * rows, latent)],
        [pltpu.VMEM((blocks * half, latent), F32)],
        1,
        "coarse_sum",
        place,
        count_into,
        pooled,
    )
    sums_other = other_core(sums)
    square = pltpu.VMEM((2 * latent, 2 * latent), F32)
    d_agg, d_direct, d_coarse, coarse_grad, node_grads = call(
        functools.partial(node_kernel, sizes),
        [
            full(count, latent),
            full(count, latent),
            full(2 * rows, latent),
            full(latent, latent),
            full(4, latent, latent),
        ],
        [square, square, square, pltpu.VMEM((rows, 2 * latent), F32)],
        6,
        "nodes",
        place,
        cells,
        agg,
        agg_other,
        sums,
        sums_other,
        upstream,
        pool_rows,
        w_coarse,
        w_self,
        w_agg,
        w_up,
        w_out,
    )
    d_pre, msg_grad = call(
        edge_back_kernel,
        [jax.ShapeDtypeStruct((edges, 2 * latent), BF16), full(latent, latent)],
        [
            pltpu.VMEM((count, 2 * latent), BF16),
            pltpu.VMEM((edges, count), BF16),
        ],
        5,
        "edges_back",
        w_msg,
        recv_rows,
        pre,
        d_agg,
    )
    edge_grads, mine_back, other_back, d_cells_own = call(
        edge_table_kernel,
        [
            full(3, latent, latent),
            full(2 * slots, latent),
            full(2 * slots, latent),
            full(count, latent),
        ],
        [pltpu.VMEM((nodes, 2 * latent), BF16)],
        8,
        "edges_table",
        place,
        cells,
        halo,
        halo_other,
        w_send,
        w_recv,
        send_rows,
        recv_rows,
        d_pre,
        msg_grad,
        d_direct,
    )
    edge_grads = edge_grads + other_core(edge_grads)
    mine = jnp.concatenate([edge_grads, coarse_grad[None]], axis=0)
    mine = jnp.where(place[1] == 0, mine, node_grads)
    share = 4 * latent // plane
    parts = exchange(mine, PLANE).reshape(plane, share, latent)
    other_back = other_core(other_back)
    d_cells_other = other_core(d_cells_own)
    (count_from,) = call(
        functools.partial(count_kernel, sizes, False),
        [full(groups, LANES)],
        [edge_keys, edge_keys],
        3,
        "count_from",
        place,
        *coarse_edges,
        after=(mine,),
    )
    copies, far_back, near_back = call(
        functools.partial(line_kernel, grad_scale),
        [
            full(line, share + coarse_block, latent),
            full(slots, latent),
            full(slots + coarse_block, latent),
        ],
        [],
        1,
        "line",
        place,
        parts,
        d_coarse,
        mine_back,
        other_back,
        after=(count_from,),
    )
    far_back = along(far_back, -2)
    back = jnp.concatenate([along(near_back, -1, True), far_back], axis=0)
    back_other = other_core(back)
    parts = exchange(copies, LINE).reshape(line, share + coarse_block, latent)
    (copies,) = call(
        functools.partial(plane_kernel, share),
        [full(plane, share + lines, latent)],
        [],
        1,
        "plane",
        parts,
    )
    packed = exchange(copies, PLANE).reshape(plane, share + lines, latent)
    (most,) = call(
        functools.partial(gather_back_kernel, (coarse_block, blocks)),
        [full(count, latent)],
        [],
        3,
        "gather_back",
        place,
        d_cells_own,
        d_cells_other,
        back,
        back_other,
        send_map,
    )
    (sums,) = call(
        functools.partial(coarse_back_sum_kernel, (coarse_block, blocks, share)),
        [full(4 * latent + rows, latent)],
        [pltpu.VMEM((blocks * half, latent), F32)],
        1,
        "coarse_back_sum",
        place,
        count_from,
        packed,
        after=(most,),
    )
    return call(
        functools.partial(finish_kernel, sizes + (pool_scale,)),
        [full(count, latent), full(8, latent, latent)],
        [],
        2,
        "finish",
        place,
        most,
        d_coarse,
        back,
        back_other,
        sums,
        other_core(sums),
        pool_rows,
    )


def solution(mesh):
    blocks, cores = mesh.devices.shape
    width = 4
    grid = mesh.devices.reshape(width, width, blocks // (width * width), cores)
    mesh = jax.sharding.Mesh(grid, SPACE + ("coarse",))
    both = SPACE + ("coarse",)
    in_specs = (
        (P(SPACE, None),)
        + (P(),) * 8
        + (P(SPACE, None), P(both), P(both), P(SPACE, None, None), P(SPACE), P("coarse"), P("coarse"))
    )
    out_specs = (P(SPACE, None), P())
    return jax.shard_map(shards, mesh=mesh, in_specs=in_specs, out_specs=out_specs, check_vma=False)
```
